512 devices in a mesh: px: 16 (over y, x), py: 32 (over z, core).
Axes of the slice: x: 4, y: 4, z: 16, core: 2. Of those that a mesh axis runs over, the one named last changes fastest.
Arguments:
- offsets: float32 [3, 64, 256, 128], P(None, 'px', 'py'), may hold values from -0.12 to 0.12
- block: float32 [48, 64, 256, 128], P(None, 'px', 'py')
- prior: float32 [48, 64, 256, 128], P(None, 'px', 'py')
Outputs:
- new_block: float32 [48, 64, 256, 128], P(None, 'px', 'py')
- search: float32 [48, 64, 256, 128], P(None, 'px', 'py')
The draws below stay inside these ranges and needn't reach their ends.
All inputs are finite; a program needn't handle non-finite values. Where the reference program divides by a largest or mean magnitude, that divisor is 1e-20 or more.
Results may differ from the reference program's by a relative error of at most 0.0003.
Values sent between devices are 32-bit elements; how exact they have to be, the bound alone decides.
No kernel may reach another device: no remote copies, remote signals or barrier semaphores. Data moves between devices by JAX's collectives and lax.ppermute only.
A program may use at most 128 MiB of HBM per device.

```python
import math
import jax
import jax.numpy as jnp
from jax import lax

CC = 128
VECS = 48
BASIS = 144
NA = 64
NB = 256
NV = 2097152


def spatial_weight():
    rise_a = jnp.exp(jnp.log(3.0) * jnp.arange(NA, dtype=jnp.float32) / (NA - 1))
    rise_b = jnp.exp(jnp.log(3.0) * jnp.arange(NB, dtype=jnp.float32) / (NB - 1))
    return rise_a[:, None, None] * rise_b[None, :, None] * jnp.ones((1, 1, CC), jnp.float32)


def wave_profile(key, length):
    freq_key, phase_key = jax.random.split(key)
    frequency = jax.random.randint(freq_key, (), 1, 4).astype(jnp.float32)
    phase = jax.random.uniform(phase_key, (), jnp.float32, -math.pi, math.pi)
    coord = jnp.arange(length, dtype=jnp.float32) / length
    return jnp.cos(math.pi * frequency * coord + phase)


def smooth_mix(key, strength):
    weight_key, scale_key, field_key = jax.random.split(key, 3)
    mixing = jax.random.normal(weight_key, (VECS, 6), jnp.float32)
    total = jnp.zeros((VECS, NA, NB, CC), jnp.float32)
    for index in range(6):
        wave_key = jax.random.fold_in(field_key, index)
        along_a = wave_profile(jax.random.fold_in(wave_key, 1), NA)
        along_b = wave_profile(jax.random.fold_in(wave_key, 2), NB)
        along_c = wave_profile(jax.random.fold_in(wave_key, 3), CC)
        field = along_a[:, None, None] * along_b[None, :, None] * along_c[None, None, :]
        total = total + mixing[:, index][:, None, None, None] * field[None]
    vector_scale = jnp.exp(jax.random.uniform(scale_key, (VECS,), jnp.float32, -0.5, 0.5))
    return (strength * total, vector_scale)


def shaped(key, noise, strength):
    smooth_part, vector_scale = smooth_mix(jax.random.fold_in(key, 5), strength)
    return vector_scale[:, None, None, None] * (noise + smooth_part) * spatial_weight()[None]


def draw_offsets(key, part):
    key = jax.random.fold_in(key, 31)
    level_key, rough_key = jax.random.split(key, 2)
    phases = jax.random.uniform(level_key, (2,), jnp.float32, -math.pi, math.pi)
    coord_a = jnp.arange(NA, dtype=jnp.float32) / NA
    coord_b = jnp.arange(NB, dtype=jnp.float32) / NB
    level = 0.5 + 0.5 * jnp.sin(2.0 * math.pi * coord_a + phases[0])[:, None] * jnp.sin(2.0 * math.pi * coord_b + phases[1])[None, :]
    amplitude = 0.03 + 0.09 * level
    rough = jax.random.uniform(rough_key, (3, NA, NB, CC), jnp.float32, -1.0, 1.0)
    return amplitude[None, :, :, None] * rough


def draw_block(key, part):
    key = jax.random.fold_in(key, 11)
    noise = jax.random.normal(key, (VECS, NA, NB, CC), jnp.float32)
    return shaped(key, noise, 2.0)


def draw_prior(key, part):
    key = jax.random.fold_in(key, 23)
    noise = jax.random.normal(key, (VECS, NA, NB, CC), jnp.float32)
    return shaped(key, noise, 2.0)


def setup_inputs(seed: int = 0) -> dict:
    key_list = jax.random.split(jax.random.key(seed), 4)
    return {
        "offsets": draw_offsets(jax.random.fold_in(key_list[3], 71), 0),
        "block": draw_block(jax.random.fold_in(key_list[3], 71), 0),
        "prior": draw_prior(jax.random.fold_in(key_list[3], 71), 0),
    }


def kuhn_tetrahedra():
    orders = [(0, 1, 2), (0, 2, 1), (1, 0, 2), (1, 2, 0), (2, 0, 1), (2, 1, 0)]
    tetrahedra = []
    for ordering in orders:
        corner = [0, 0, 0]
        corners = [(0, 0, 0)]
        for axis_step in ordering:
            corner[axis_step] = 1
            corners.append((corner[0], corner[1], corner[2]))
        tetrahedra.append(corners)
    return tetrahedra

def stencil_offsets():
    distinct = []
    for corners in kuhn_tetrahedra():
        for first_corner in corners:
            for second_corner in corners:
                shift_key = (second_corner[0] - first_corner[0], second_corner[1] - first_corner[1], second_corner[2] - first_corner[2])
                if shift_key not in distinct:
                    distinct.append(shift_key)
    return sorted(distinct)

def corner_slice(positions, corner):
    cells_a = positions.shape[1] - 1
    cells_b = positions.shape[2] - 1
    depth = positions.shape[3]
    return positions[:, corner[0]:corner[0] + cells_a, corner[1]:corner[1] + cells_b, corner[2]:corner[2] + depth - 1]

def placed_at(entry_value, corner):
    return jnp.pad(entry_value, ((corner[0], 1 - corner[0]), (corner[1], 1 - corner[1]), (corner[2], 1 - corner[2])))

def assemble(positions, cell_valid):
    offsets_list = stencil_offsets()
    full_shape = positions.shape[1:]
    inside = cell_valid[:, :, None]
    entry_sums = {}
    mass_sums = {}
    for corners in kuhn_tetrahedra():
        anchor = corner_slice(positions, corners[0])
        edge_one = corner_slice(positions, corners[1]) - anchor
        edge_two = corner_slice(positions, corners[2]) - anchor
        edge_three = corner_slice(positions, corners[3]) - anchor
        grad_one = jnp.cross(edge_two, edge_three, axis=0)
        grad_two = jnp.cross(edge_three, edge_one, axis=0)
        grad_three = jnp.cross(edge_one, edge_two, axis=0)
        gradients = [-(grad_one + grad_two + grad_three), grad_one, grad_two, grad_three]
        determinant = lax.optimization_barrier(jnp.sum(edge_one * grad_one, axis=0))
        volume_six = jnp.where(inside, jnp.abs(determinant), 1.0)
        weight = jnp.where(inside, 1.0 / (6.0 * volume_six), 0.0)
        for first in range(4):
            for second in range(4):
                entry_value = lax.optimization_barrier(jnp.sum(gradients[first] * gradients[second], axis=0)) * weight
                shift_key = (corners[second][0] - corners[first][0], corners[second][1] - corners[first][1], corners[second][2] - corners[first][2])
                slot_key = (corners[first], offsets_list.index(shift_key))
                if slot_key in entry_sums:
                    entry_sums[slot_key] = entry_sums[slot_key] + entry_value
                else:
                    entry_sums[slot_key] = entry_value
        portion = jnp.where(inside, volume_six / 24.0, 0.0)
        for corner in corners:
            if corner in mass_sums:
                mass_sums[corner] = mass_sums[corner] + portion
            else:
                mass_sums[corner] = portion
    totals = [jnp.zeros(full_shape, jnp.float32) for entry in offsets_list]
    for slot_key in entry_sums:
        totals[slot_key[1]] = totals[slot_key[1]] + placed_at(entry_sums[slot_key], slot_key[0])
    mass_total = jnp.zeros(full_shape, jnp.float32)
    for corner in mass_sums:
        mass_total = mass_total + placed_at(mass_sums[corner], corner)
    coefs = jnp.stack([entry[1:-1, 1:-1, :] for entry in totals])
    return (coefs, mass_total[1:-1, 1:-1, :])

def window_positions(extended_offsets, index_a, index_b):
    depth = extended_offsets.shape[3]
    grid_a = jnp.broadcast_to(index_a.astype(jnp.float32)[:, None, None], extended_offsets.shape[1:])
    grid_b = jnp.broadcast_to(index_b.astype(jnp.float32)[None, :, None], extended_offsets.shape[1:])
    grid_c = jnp.broadcast_to(jnp.arange(depth, dtype=jnp.int32).astype(jnp.float32)[None, None, :], extended_offsets.shape[1:])
    return jnp.stack([grid_a, grid_b, grid_c]) + extended_offsets

def stiffness_apply(extended, coefs):
    offsets_list = stencil_offsets()
    rows_a = extended.shape[1] - 2
    rows_b = extended.shape[2] - 2
    depth = extended.shape[3]
    padded = jnp.pad(extended, ((0, 0), (0, 0), (0, 0), (1, 1)))
    result = jnp.zeros((extended.shape[0], rows_a, rows_b, depth), jnp.float32)
    for position, shift_key in enumerate(offsets_list):
        result = result + coefs[position] * padded[:, 1 + shift_key[0]:1 + shift_key[0] + rows_a, 1 + shift_key[1]:1 + shift_key[1] + rows_b, 1 + shift_key[2]:1 + shift_key[2] + depth]
    return result

def ritz(gram_k, gram_m, vecs):
    lower = jnp.linalg.cholesky(gram_m)
    half = jax.scipy.linalg.solve_triangular(lower, gram_k, lower=True)
    reduced = jax.scipy.linalg.solve_triangular(lower, half.T, lower=True)
    bound = jnp.max(lax.optimization_barrier(jnp.sum(jnp.abs(reduced), axis=1)))
    shifted = jnp.eye(reduced.shape[0], dtype=jnp.float32) - reduced / bound
    filtered = jnp.dot(shifted, shifted[:, :vecs], precision=lax.Precision.HIGHEST)
    return jax.scipy.linalg.solve_triangular(lower, filtered, lower=True, trans=1)

def global_apply(fields, coefs):
    padded = jnp.pad(fields, ((0, 0), (1, 1), (1, 1), (0, 0)))
    return stiffness_apply(padded, coefs)

def reference(offsets, block, prior):
    padded_offsets = jnp.pad(offsets, ((0, 0), (1, 1), (1, 1), (0, 0)))
    index_a = jnp.arange(NA + 2, dtype=jnp.int32) - 1
    index_b = jnp.arange(NB + 2, dtype=jnp.int32) - 1
    positions = window_positions(padded_offsets, index_a, index_b)
    cells_a = index_a[:-1]
    cells_b = index_b[:-1]
    valid_a = (cells_a >= 0) & (cells_a <= NA - 2)
    valid_b = (cells_b >= 0) & (cells_b <= NB - 2)
    coefs, mass = assemble(positions, valid_a[:, None] & valid_b[None, :])
    diagonal = coefs[stencil_offsets().index((0, 0, 0))]
    k_block = global_apply(block, coefs)
    m_block = mass * block
    numer = lax.optimization_barrier(jnp.sum(block * k_block, axis=(1, 2, 3)))
    denom = lax.optimization_barrier(jnp.sum(block * m_block, axis=(1, 2, 3)))
    quotient = numer / denom
    search = (k_block - quotient[:, None, None, None] * m_block) / diagonal
    k_search = global_apply(search, coefs)
    k_prior = global_apply(prior, coefs)
    basis = jnp.concatenate([block, search, prior]).reshape(BASIS, -1)
    k_basis = jnp.concatenate([k_block, k_search, k_prior]).reshape(BASIS, -1)
    m_basis = basis * mass.reshape(1, -1)
    gram_k = lax.dot_general(basis, k_basis, (((1,), (1,)), ((), ())), precision=lax.Precision.HIGHEST)
    gram_m = lax.dot_general(basis, m_basis, (((1,), (1,)), ((), ())), precision=lax.Precision.HIGHEST)
    coeffs = ritz(gram_k, gram_m, VECS)
    scale = jnp.sqrt(jnp.float32(NV))
    new_block = scale * lax.dot_general(coeffs, basis, (((0,), (0,)), ((), ())), precision=lax.Precision.HIGHEST)
    return (new_block.reshape(block.shape), search)
```

```python
import jax
import jax.numpy as jnp
from jax import lax
from jax.sharding import Mesh
from jax.sharding import PartitionSpec as P


def padded_2(cells, sides, width):
    for axis, dim in sides:
        count = lax.axis_size(axis)
        ends = count - 1
        head = lax.slice_in_dim(cells, 0, width, axis=dim)
        tail = lax.slice_in_dim(cells, cells.shape[dim] - width, cells.shape[dim], axis=dim)
        cells = jnp.concatenate(
            [
                lax.ppermute(tail, axis, [(i, (i + 1) % count) for i in range(ends)]),
                cells,
                lax.ppermute(head, axis, [((i + 1) % count, i) for i in range(ends)]),
            ],
            axis=dim,
        )
    return cells


def kuhn_tetrahedra():
    orders = [(0, 1, 2), (0, 2, 1), (1, 0, 2), (1, 2, 0), (2, 0, 1), (2, 1, 0)]
    tetrahedra = []
    for ordering in orders:
        corner = [0, 0, 0]
        corners = [(0, 0, 0)]
        for axis_step in ordering:
            corner[axis_step] = 1
            corners.append((corner[0], corner[1], corner[2]))
        tetrahedra.append(corners)
    return tetrahedra


def stencil_offsets():
    distinct = []
    for corners in kuhn_tetrahedra():
        for first_corner in corners:
            for second_corner in corners:
                shift_key = (
                    second_corner[0] - first_corner[0],
                    second_corner[1] - first_corner[1],
                    second_corner[2] - first_corner[2],
                )
                if shift_key not in distinct:
                    distinct.append(shift_key)
    return sorted(distinct)


def corner_slice(positions, corner):
    cells_a = positions.shape[1] - 1
    cells_b = positions.shape[2] - 1
    depth = positions.shape[3]
    return positions[
        :,
        corner[0] : corner[0] + cells_a,
        corner[1] : corner[1] + cells_b,
        corner[2] : corner[2] + depth - 1,
    ]


def placed_at(entry_value, corner):
    return jnp.pad(
        entry_value,
        ((corner[0], 1 - corner[0]), (corner[1], 1 - corner[1]), (corner[2], 1 - corner[2])),
    )


def assemble(positions, cell_valid):
    offsets_list = stencil_offsets()
    full_shape = positions.shape[1:]
    inside = cell_valid[:, :, None]
    entry_sums = {}
    mass_sums = {}
    for corners in kuhn_tetrahedra():
        anchor = corner_slice(positions, corners[0])
        edge_one = corner_slice(positions, corners[1]) - anchor
        edge_two = corner_slice(positions, corners[2]) - anchor
        edge_three = corner_slice(positions, corners[3]) - anchor
        grad_one = jnp.cross(edge_two, edge_three, axis=0)
        grad_two = jnp.cross(edge_three, edge_one, axis=0)
        grad_three = jnp.cross(edge_one, edge_two, axis=0)
        gradients = [-(grad_one + grad_two + grad_three), grad_one, grad_two, grad_three]
        determinant = jnp.sum(edge_one * grad_one, axis=0)
        volume_six = jnp.where(inside, jnp.abs(determinant), 1.0)
        weight = jnp.where(inside, 1.0 / (6.0 * volume_six), 0.0)
        for first in range(4):
            for second in range(4):
                entry_value = jnp.sum(gradients[first] * gradients[second], axis=0) * weight
                shift_key = (
                    corners[second][0] - corners[first][0],
                    corners[second][1] - corners[first][1],
                    corners[second][2] - corners[first][2],
                )
                slot_key = (corners[first], offsets_list.index(shift_key))
                if slot_key in entry_sums:
                    entry_sums[slot_key] = entry_sums[slot_key] + entry_value
                else:
                    entry_sums[slot_key] = entry_value
        portion = jnp.where(inside, volume_six / 24.0, 0.0)
        for corner in corners:
            if corner in mass_sums:
                mass_sums[corner] = mass_sums[corner] + portion
            else:
                mass_sums[corner] = portion
    totals = [jnp.zeros(full_shape, jnp.float32) for entry in offsets_list]
    for slot_key in entry_sums:
        totals[slot_key[1]] = totals[slot_key[1]] + placed_at(entry_sums[slot_key], slot_key[0])
    mass_total = jnp.zeros(full_shape, jnp.float32)
    for corner in mass_sums:
        mass_total = mass_total + placed_at(mass_sums[corner], corner)
    coefs = jnp.stack([entry[1:-1, 1:-1, :] for entry in totals])
    return (coefs, mass_total[1:-1, 1:-1, :])


def window_positions(extended_offsets, index_a, index_b):
    depth = extended_offsets.shape[3]
    grid_a = jnp.broadcast_to(
        index_a.astype(jnp.float32)[:, None, None], extended_offsets.shape[1:]
    )
    grid_b = jnp.broadcast_to(
        index_b.astype(jnp.float32)[None, :, None], extended_offsets.shape[1:]
    )
    grid_c = jnp.broadcast_to(
        jnp.arange(depth, dtype=jnp.int32).astype(jnp.float32)[None, None, :],
        extended_offsets.shape[1:],
    )
    return jnp.stack([grid_a, grid_b, grid_c]) + extended_offsets


def stiffness_apply(extended, coefs):
    offsets_list = stencil_offsets()
    rows_a = extended.shape[1] - 2
    rows_b = extended.shape[2] - 2
    depth = extended.shape[3]
    padded = jnp.pad(extended, ((0, 0), (0, 0), (0, 0), (1, 1)))
    result = jnp.zeros((extended.shape[0], rows_a, rows_b, depth), jnp.float32)
    for position, shift_key in enumerate(offsets_list):
        result = (
            result
            + coefs[position]
            * padded[
                :,
                1 + shift_key[0] : 1 + shift_key[0] + rows_a,
                1 + shift_key[1] : 1 + shift_key[1] + rows_b,
                1 + shift_key[2] : 1 + shift_key[2] + depth,
            ]
        )
    return result


def ritz(gram_k, gram_m, vecs):
    lower = jnp.linalg.cholesky(gram_m)
    half = jax.scipy.linalg.solve_triangular(lower, gram_k, lower=True)
    reduced = jax.scipy.linalg.solve_triangular(lower, half.T, lower=True)
    bound = jnp.max(jnp.sum(jnp.abs(reduced), axis=1))
    shifted = jnp.eye(reduced.shape[0], dtype=jnp.float32) - reduced / bound
    filtered = jnp.dot(shifted, shifted[:, :vecs], precision=lax.Precision.HIGHEST)
    return jax.scipy.linalg.solve_triangular(lower, filtered, lower=True, trans=1)


def local_grams(vectors, k_vectors, mass):
    flat = vectors.reshape(vectors.shape[0], -1)
    k_flat = k_vectors.reshape(vectors.shape[0], -1)
    m_flat = flat * mass.reshape(1, -1)
    gram_k = lax.dot_general(
        flat, k_flat, (((1,), (1,)), ((), ())), precision=lax.Precision.HIGHEST
    )
    gram_m = lax.dot_general(
        flat, m_flat, (((1,), (1,)), ((), ())), precision=lax.Precision.HIGHEST
    )
    return (gram_k, gram_m)


def spread_sum(rows):
    plane = ("px", "pc")
    count = lax.axis_size("px") * lax.axis_size("pc")
    depth = lax.axis_size("pz")
    pieces = rows.reshape(count, -1, rows.shape[1])
    part = jnp.sum(lax.all_to_all(pieces, plane, 0, 0), axis=0)
    part = jnp.sum(
        lax.all_to_all(jnp.broadcast_to(part[None], (depth,) + part.shape), "pz", 0, 0), axis=0
    )
    whole = lax.all_to_all(jnp.broadcast_to(part[None], (count,) + part.shape), plane, 0, 0)
    return whole.reshape(rows.shape)


def copied_sum(part):
    for axes in (("px", "pc"), ("pz",)):
        count = 1
        for axis in axes:
            count = count * lax.axis_size(axis)
        part = jnp.sum(
            lax.all_to_all(jnp.broadcast_to(part[None], (count,) + part.shape), axes, 0, 0), axis=0
        )
    return part


def packed_grams(gram_k, gram_m):
    order = gram_k.shape[0]
    upper = jnp.triu(gram_k) + jnp.tril(gram_m, -1)
    flat = jnp.concatenate([upper.reshape(-1), jnp.diagonal(gram_m)])
    size = -(-flat.shape[0] // 32768) * 32768
    flat = jnp.pad(flat, (0, size - flat.shape[0]))
    total = spread_sum(flat.reshape(-1, 128)).reshape(-1)
    square = total[: order * order].reshape(order, order)
    diagonal = total[order * order : order * order + order]
    high = jnp.triu(square)
    low = jnp.tril(square, -1)
    return (high + jnp.triu(square, 1).T, low + low.T + jnp.diag(diagonal))


def shards(offsets, block, prior):
    vecs = block.shape[0]
    rows_a = block.shape[1]
    rows_b = block.shape[2]
    depth = block.shape[3]
    total_a = rows_a * lax.axis_size("px")
    total_b = rows_b * lax.axis_size(("pz", "pc"))
    start_a = lax.axis_index("px") * rows_a
    start_b = lax.axis_index(("pz", "pc")) * rows_b
    extended_offsets = padded_2(offsets, (("px", 1), (("pz", "pc"), 2)), 2)
    index_a = start_a - 2 + jnp.arange(rows_a + 4, dtype=jnp.int32)
    index_b = start_b - 2 + jnp.arange(rows_b + 4, dtype=jnp.int32)
    positions = window_positions(extended_offsets, index_a, index_b)
    cells_a = index_a[:-1]
    cells_b = index_b[:-1]
    valid_a = (cells_a >= 0) & (cells_a <= total_a - 2)
    valid_b = (cells_b >= 0) & (cells_b <= total_b - 2)
    coefs_wide, mass_wide = assemble(positions, valid_a[:, None] & valid_b[None, :])
    coefs = coefs_wide[:, 1:-1, 1:-1, :]
    mass = mass_wide[1:-1, 1:-1, :]
    centre = stencil_offsets().index((0, 0, 0))
    diagonal = coefs[centre]
    first_rim = padded_2(block, (("px", 1), (("pz", "pc"), 2)), 1)
    k_block = stiffness_apply(first_rim, coefs)
    m_block = mass * block
    sums = jnp.stack(
        [jnp.sum(block * k_block, axis=(1, 2, 3)), jnp.sum(block * m_block, axis=(1, 2, 3))]
    )
    sums = copied_sum(jnp.pad(sums, ((0, 6), (0, 128 - vecs))))
    numer = sums[0, :vecs]
    denom = sums[1, :vecs]
    quotient = numer / denom
    search = (k_block - quotient[:, None, None, None] * m_block) / diagonal
    second_rim = padded_2(jnp.concatenate([search, prior]), (("px", 1), (("pz", "pc"), 2)), 1)
    applied = stiffness_apply(second_rim, coefs)
    k_search = applied[:vecs]
    k_prior = applied[vecs:]
    basis = jnp.concatenate([block, search, prior])
    k_basis = jnp.concatenate([k_block, k_search, k_prior])
    gram_k, gram_m = packed_grams(*local_grams(basis, k_basis, mass))
    coeffs = ritz(gram_k, gram_m, vecs)
    scale = jnp.sqrt(jnp.float32(total_a * total_b * depth))
    flat_basis = basis.reshape(basis.shape[0], -1)
    new_block = scale * lax.dot_general(
        coeffs, flat_basis, (((0,), (0,)), ((), ())), precision=lax.Precision.HIGHEST
    )
    return (new_block.reshape(block.shape), search)


def solution(mesh):
    grid = Mesh(
        mesh.devices.reshape(mesh.shape["px"], mesh.shape["py"] // 2, 2), ("px", "pz", "pc")
    )
    spec = P(None, "px", ("pz", "pc"), None)
    return jax.shard_map(
        shards, mesh=grid, in_specs=(spec, spec, spec), out_specs=(spec, spec), check_vma=False
    )
```

```python
import jax
import jax.numpy as jnp
from jax import lax
from jax.sharding import Mesh
from jax.sharding import PartitionSpec as P


def padded_2(cells, sides, width):
    for axis, dim in sides:
        count = lax.axis_size(axis)
        ends = count - 1
        head = lax.slice_in_dim(cells, 0, width, axis=dim)
        tail = lax.slice_in_dim(cells, cells.shape[dim] - width, cells.shape[dim], axis=dim)
        cells = jnp.concatenate(
            [
                lax.ppermute(tail, axis, [(i, (i + 1) % count) for i in range(ends)]),
                cells,
                lax.ppermute(head, axis, [((i + 1) % count, i) for i in range(ends)]),
            ],
            axis=dim,
        )
    return cells


def kuhn_tetrahedra():
    orders = [(0, 1, 2), (0, 2, 1), (1, 0, 2), (1, 2, 0), (2, 0, 1), (2, 1, 0)]
    tetrahedra = []
    for ordering in orders:
        corner = [0, 0, 0]
        corners = [(0, 0, 0)]
        for axis_step in ordering:
            corner[axis_step] = 1
            corners.append((corner[0], corner[1], corner[2]))
        tetrahedra.append(corners)
    return tetrahedra


def stencil_offsets():
    distinct = []
    for corners in kuhn_tetrahedra():
        for first_corner in corners:
            for second_corner in corners:
                shift_key = (
                    second_corner[0] - first_corner[0],
                    second_corner[1] - first_corner[1],
                    second_corner[2] - first_corner[2],
                )
                if shift_key not in distinct:
                    distinct.append(shift_key)
    return sorted(distinct)


def corner_slice(positions, corner):
    cells_a = positions.shape[1] - 1
    cells_b = positions.shape[2] - 1
    depth = positions.shape[3]
    return positions[
        :,
        corner[0] : corner[0] + cells_a,
        corner[1] : corner[1] + cells_b,
        corner[2] : corner[2] + depth - 1,
    ]


def placed_at(entry_value, corner):
    return jnp.pad(
        entry_value,
        ((corner[0], 1 - corner[0]), (corner[1], 1 - corner[1]), (corner[2], 1 - corner[2])),
    )


def assemble(positions, cell_valid):
    offsets_list = stencil_offsets()
    full_shape = positions.shape[1:]
    inside = cell_valid[:, :, None]
    entry_sums = {}
    mass_sums = {}
    for corners in kuhn_tetrahedra():
        anchor = corner_slice(positions, corners[0])
        edge_one = corner_slice(positions, corners[1]) - anchor
        edge_two = corner_slice(positions, corners[2]) - anchor
        edge_three = corner_slice(positions, corners[3]) - anchor
        grad_one = jnp.cross(edge_two, edge_three, axis=0)
        grad_two = jnp.cross(edge_three, edge_one, axis=0)
        grad_three = jnp.cross(edge_one, edge_two, axis=0)
        gradients = [-(grad_one + grad_two + grad_three), grad_one, grad_two, grad_three]
        determinant = jnp.sum(edge_one * grad_one, axis=0)
        volume_six = jnp.where(inside, jnp.abs(determinant), 1.0)
        weight = jnp.where(inside, 1.0 / (6.0 * volume_six), 0.0)
        for first in range(4):
            for second in range(4):
                entry_value = jnp.sum(gradients[first] * gradients[second], axis=0) * weight
                shift_key = (
                    corners[second][0] - corners[first][0],
                    corners[second][1] - corners[first][1],
                    corners[second][2] - corners[first][2],
                )
                slot_key = (corners[first], offsets_list.index(shift_key))
                if slot_key in entry_sums:
                    entry_sums[slot_key] = entry_sums[slot_key] + entry_value
                else:
                    entry_sums[slot_key] = entry_value
        portion = jnp.where(inside, volume_six / 24.0, 0.0)
        for corner in corners:
            if corner in mass_sums:
                mass_sums[corner] = mass_sums[corner] + portion
            else:
                mass_sums[corner] = portion
    totals = [jnp.zeros(full_shape, jnp.float32) for entry in offsets_list]
    for slot_key in entry_sums:
        totals[slot_key[1]] = totals[slot_key[1]] + placed_at(entry_sums[slot_key], slot_key[0])
    mass_total = jnp.zeros(full_shape, jnp.float32)
    for corner in mass_sums:
        mass_total = mass_total + placed_at(mass_sums[corner], corner)
    coefs = jnp.stack([entry[1:-1, 1:-1, :] for entry in totals])
    return (coefs, mass_total[1:-1, 1:-1, :])


def window_positions(extended_offsets, index_a, index_b):
    depth = extended_offsets.shape[3]
    grid_a = jnp.broadcast_to(
        index_a.astype(jnp.float32)[:, None, None], extended_offsets.shape[1:]
    )
    grid_b = jnp.broadcast_to(
        index_b.astype(jnp.float32)[None, :, None], extended_offsets.shape[1:]
    )
    grid_c = jnp.broadcast_to(
        jnp.arange(depth, dtype=jnp.int32).astype(jnp.float32)[None, None, :],
        extended_offsets.shape[1:],
    )
    return jnp.stack([grid_a, grid_b, grid_c]) + extended_offsets


def stiffness_apply(extended, coefs):
    offsets_list = stencil_offsets()
    rows_a = extended.shape[1] - 2
    rows_b = extended.shape[2] - 2
    depth = extended.shape[3]
    padded = jnp.pad(extended, ((0, 0), (0, 0), (0, 0), (1, 1)))
    result = jnp.zeros((extended.shape[0], rows_a, rows_b, depth), jnp.float32)
    for position, shift_key in enumerate(offsets_list):
        result = (
            result
            + coefs[position]
            * padded[
                :,
                1 + shift_key[0] : 1 + shift_key[0] + rows_a,
                1 + shift_key[1] : 1 + shift_key[1] + rows_b,
                1 + shift_key[2] : 1 + shift_key[2] + depth,
            ]
        )
    return result


def ritz(gram_k, gram_m, vecs):
    lower = jnp.linalg.cholesky(gram_m)
    half = jax.scipy.linalg.solve_triangular(lower, gram_k, lower=True)
    reduced = jax.scipy.linalg.solve_triangular(lower, half.T, lower=True)
    bound = jnp.max(jnp.sum(jnp.abs(reduced), axis=1))
    shifted = jnp.eye(reduced.shape[0], dtype=jnp.float32) - reduced / bound
    filtered = jnp.dot(shifted, shifted[:, :vecs], precision=lax.Precision.HIGHEST)
    return jax.scipy.linalg.solve_triangular(lower, filtered, lower=True, trans=1)


def local_grams(vectors, k_vectors, mass):
    flat = vectors.reshape(vectors.shape[0], -1)
    k_flat = k_vectors.reshape(vectors.shape[0], -1)
    m_flat = flat * mass.reshape(1, -1)
    gram_k = lax.dot_general(
        flat, k_flat, (((1,), (1,)), ((), ())), precision=lax.Precision.HIGHEST
    )
    gram_m = lax.dot_general(
        flat, m_flat, (((1,), (1,)), ((), ())), precision=lax.Precision.HIGHEST
    )
    return (gram_k, gram_m)


def spread_sum(rows):
    plane = ("px", "pc")
    count = lax.axis_size("px") * lax.axis_size("pc")
    depth = lax.axis_size("pz")
    pieces = rows.reshape(count, -1, rows.shape[1])
    part = jnp.sum(lax.all_to_all(pieces, plane, 0, 0), axis=0)
    part = jnp.sum(
        lax.all_to_all(jnp.broadcast_to(part[None], (depth,) + part.shape), "pz", 0, 0), axis=0
    )
    whole = lax.all_to_all(jnp.broadcast_to(part[None], (count,) + part.shape), plane, 0, 0)
    return whole.reshape(rows.shape)


def summed_grams(gram_k, gram_m):
    order = gram_k.shape[0]
    eye = jnp.eye(order, dtype=jnp.bool_)
    square = jnp.triu(gram_k) + jnp.tril(gram_m, -1)
    diagonal = jnp.sum(jnp.where(eye, gram_m, 0.0), axis=0)
    rows = jnp.concatenate([square, jnp.broadcast_to(diagonal[None], (256 - order, order))])
    total = spread_sum(jnp.pad(rows, ((0, 0), (0, 256 - order))))
    square = total[:order, :order]
    diagonal = total[order, :order]
    high = jnp.triu(square)
    low = jnp.tril(square, -1)
    return (high + jnp.triu(square, 1).T, low + low.T + jnp.where(eye, diagonal[None], 0.0))


def combined(gram, quotient):
    vecs = quotient.shape[0]
    rows = jnp.concatenate(
        [
            gram[:vecs],
            gram[vecs : 2 * vecs] - quotient[:, None] * gram[2 * vecs : 3 * vecs],
            gram[3 * vecs :],
        ]
    )
    return jnp.concatenate(
        [
            rows[:, :vecs],
            rows[:, vecs : 2 * vecs] - quotient[None, :] * rows[:, 2 * vecs : 3 * vecs],
            rows[:, 3 * vecs :],
        ],
        axis=1,
    )


def shards(offsets, block, prior):
    vecs = block.shape[0]
    rows_a = block.shape[1]
    rows_b = block.shape[2]
    depth = block.shape[3]
    total_a = rows_a * lax.axis_size("px")
    total_b = rows_b * lax.axis_size(("pz", "pc"))
    start_a = lax.axis_index("px") * rows_a
    start_b = lax.axis_index(("pz", "pc")) * rows_b
    sides = (("px", 1), (("pz", "pc"), 2))
    wide = padded_2(jnp.concatenate([offsets, block]), sides, 2)
    prior_wide = padded_2(prior, sides, 1)
    extended_offsets = wide[: offsets.shape[0]]
    block_wide = wide[offsets.shape[0] :]
    index_a = start_a - 2 + jnp.arange(rows_a + 4, dtype=jnp.int32)
    index_b = start_b - 2 + jnp.arange(rows_b + 4, dtype=jnp.int32)
    positions = window_positions(extended_offsets, index_a, index_b)
    cells_a = index_a[:-1]
    cells_b = index_b[:-1]
    valid_a = (cells_a >= 0) & (cells_a <= total_a - 2)
    valid_b = (cells_b >= 0) & (cells_b <= total_b - 2)
    coefs_wide, mass_wide = assemble(positions, valid_a[:, None] & valid_b[None, :])
    coefs = coefs_wide[:, 1:-1, 1:-1, :]
    mass = mass_wide[1:-1, 1:-1, :]
    centre = stencil_offsets().index((0, 0, 0))
    vertex_a = index_a[1:-1]
    vertex_b = index_b[1:-1]
    inside_a = (vertex_a >= 0) & (vertex_a <= total_a - 1)
    inside_b = (vertex_b >= 0) & (vertex_b <= total_b - 1)
    inside = (inside_a[:, None] & inside_b[None, :])[:, :, None]
    diagonal = jnp.where(inside, coefs_wide[centre], 1.0)
    k_wide = stiffness_apply(block_wide, coefs_wide)
    u_wide = k_wide / diagonal
    w_wide = mass_wide * block_wide[:, 1:-1, 1:-1, :] / diagonal
    applied = stiffness_apply(jnp.concatenate([u_wide, w_wide, prior_wide]), coefs)
    u_part = u_wide[:, 1:-1, 1:-1, :]
    w_part = w_wide[:, 1:-1, 1:-1, :]
    basis = jnp.concatenate([block, u_part, w_part, prior])
    k_basis = jnp.concatenate([k_wide[:, 1:-1, 1:-1, :], applied])
    gram_k, gram_m = summed_grams(*local_grams(basis, k_basis, mass))
    quotient = jnp.diagonal(gram_k[:vecs, :vecs]) / jnp.diagonal(gram_m[:vecs, :vecs])
    search = u_part - quotient[:, None, None, None] * w_part
    coeffs = ritz(combined(gram_k, quotient), combined(gram_m, quotient), vecs)
    scale = jnp.sqrt(jnp.float32(total_a * total_b * depth))
    flat_basis = jnp.concatenate([block, search, prior]).reshape(3 * vecs, -1)
    new_block = scale * lax.dot_general(
        coeffs, flat_basis, (((0,), (0,)), ((), ())), precision=lax.Precision.HIGHEST
    )
    return (new_block.reshape(block.shape), search)


def solution(mesh):
    grid = Mesh(
        mesh.devices.reshape(mesh.shape["px"], mesh.shape["py"] // 2, 2), ("px", "pz", "pc")
    )
    spec = P(None, "px", ("pz", "pc"), None)
    return jax.shard_map(
        shards, mesh=grid, in_specs=(spec, spec, spec), out_specs=(spec, spec), check_vma=False
    )
```

```python
import jax
import jax.numpy as jnp
from jax import lax
from jax.experimental import pallas as pl
from jax.experimental.pallas import tpu as pltpu
from jax.sharding import Mesh
from jax.sharding import PartitionSpec as P


VECS = 48
HI = lax.Precision.HIGHEST


def dots(a, b, dims):
    return lax.dot_general(a, b, (dims, ((), ())), precision=HI, preferred_element_type=jnp.float32)


def eliminated(gram):
    order = gram.shape[0]
    third = order // 3
    rows = lax.broadcasted_iota(jnp.int32, gram.shape, 0)
    cols = lax.broadcasted_iota(jnp.int32, gram.shape, 1)
    inverse = jnp.where(rows == cols, 1.0, 0.0).astype(jnp.float32)
    place = lax.broadcasted_iota(jnp.int32, (third, 128), 0)
    done = []
    for j in range(3):
        left = gram[:third]
        right = inverse[:third]
        gram = gram[third:]
        inverse = inverse[third:]
        pivots = jnp.ones((third, 128), jnp.float32)
        for k in range(third):
            c = third * j + k
            column = jnp.broadcast_to(left[:, c : c + 1], (third, 128))
            pivot = column[k : k + 1, :]
            pivots = jnp.where(place == k, pivot, pivots)
            factor = jnp.where(place > k, column * (1.0 / pivot), 0.0)
            factor = jnp.concatenate([factor, factor], axis=1)
            left, right = (
                left - factor * left[k : k + 1, :],
                right - factor * right[k : k + 1, :],
            )
        scale = 1.0 / jnp.sqrt(pivots)
        scale = jnp.concatenate([scale, scale], axis=1)
        left = left * scale
        right = right * scale
        done.append(right)
        if j < 2:
            flipped = left.T[third * (j + 1) : order]
            gram = gram - dots(flipped, left, ((1,), (0,)))
            inverse = inverse - dots(flipped, right, ((1,), (0,)))
    return jnp.concatenate(done, axis=0)


def ritz_core(total):
    vecs = VECS
    order = 3 * vecs
    full = 4 * vecs
    rows = lax.broadcasted_iota(jnp.int32, total.shape, 0)
    cols = lax.broadcasted_iota(jnp.int32, total.shape, 1)
    flipped = total.T
    diagonal = total[full : full + 1, :]
    gram_k = jnp.where(rows <= cols, total, flipped)
    gram_m = jnp.where(rows > cols, total, jnp.where(rows == cols, diagonal, flipped))
    eye = rows == cols
    top = lambda g: jnp.sum(jnp.where(eye, g, 0.0)[:vecs], axis=1, keepdims=True)
    quotient = top(gram_k) / top(gram_m)

    def joined(g):
        mid = g[vecs : 2 * vecs] - quotient * g[2 * vecs : 3 * vecs]
        return jnp.concatenate([g[:vecs], mid, g[3 * vecs : full]], axis=0)

    gram_k = joined(joined(gram_k).T)
    gram_m = joined(joined(gram_m).T)
    gram_m = jnp.concatenate([gram_m, jnp.zeros((order, 256 - order), jnp.float32)], axis=1)
    inverse = eliminated(gram_m)[:, :order]
    half = dots(inverse, gram_k, ((1,), (0,)))
    reduced = dots(half, inverse, ((1,), (1,)))
    bound = jnp.max(jnp.sum(jnp.abs(reduced), axis=1, keepdims=True), axis=0, keepdims=True)
    eye = lax.broadcasted_iota(jnp.int32, (order, order), 0) == lax.broadcasted_iota(
        jnp.int32, (order, order), 1
    )
    shifted = jnp.where(eye, 1.0, 0.0) - reduced / bound
    filtered = dots(shifted[:vecs], shifted, ((1,), (0,)))
    return dots(filtered, inverse, ((1,), (0,))), quotient


def ritz_kernel(total_ref, coeffs_ref, quotient_ref):
    coeffs, quotient = ritz_core(total_ref[...])
    coeffs_ref[...] = coeffs
    quotient_ref[...] = jnp.broadcast_to(quotient, quotient_ref.shape)


def ritz_call(total):
    return pl.pallas_call(
        ritz_kernel,
        out_shape=(
            jax.ShapeDtypeStruct((VECS, 3 * VECS), jnp.float32),
            jax.ShapeDtypeStruct((VECS, 128), jnp.float32),
        ),
        in_specs=[pl.BlockSpec(memory_space=pltpu.VMEM)],
        out_specs=(pl.BlockSpec(memory_space=pltpu.VMEM),) * 2,
        compiler_params=pltpu.CompilerParams(vmem_limit_bytes=32 * 2**20),
    )(total)


def padded_2(cells, sides, width):
    for axis, dim in sides:
        count = lax.axis_size(axis)
        ends = count - 1
        head = lax.slice_in_dim(cells, 0, width, axis=dim)
        tail = lax.slice_in_dim(cells, cells.shape[dim] - width, cells.shape[dim], axis=dim)
        cells = jnp.concatenate(
            [
                lax.ppermute(tail, axis, [(i, (i + 1) % count) for i in range(ends)]),
                cells,
                lax.ppermute(head, axis, [((i + 1) % count, i) for i in range(ends)]),
            ],
            axis=dim,
        )
    return cells


def kuhn_tetrahedra():
    orders = [(0, 1, 2), (0, 2, 1), (1, 0, 2), (1, 2, 0), (2, 0, 1), (2, 1, 0)]
    tetrahedra = []
    for ordering in orders:
        corner = [0, 0, 0]
        corners = [(0, 0, 0)]
        for axis_step in ordering:
            corner[axis_step] = 1
            corners.append((corner[0], corner[1], corner[2]))
        tetrahedra.append(corners)
    return tetrahedra


def stencil_offsets():
    distinct = []
    for corners in kuhn_tetrahedra():
        for first_corner in corners:
            for second_corner in corners:
                shift_key = (
                    second_corner[0] - first_corner[0],
                    second_corner[1] - first_corner[1],
                    second_corner[2] - first_corner[2],
                )
                if shift_key not in distinct:
                    distinct.append(shift_key)
    return sorted(distinct)


def corner_slice(positions, corner):
    cells_a = positions.shape[1] - 1
    cells_b = positions.shape[2] - 1
    depth = positions.shape[3]
    return positions[
        :,
        corner[0] : corner[0] + cells_a,
        corner[1] : corner[1] + cells_b,
        corner[2] : corner[2] + depth - 1,
    ]


def placed_at(entry_value, corner):
    return jnp.pad(
        entry_value,
        ((corner[0], 1 - corner[0]), (corner[1], 1 - corner[1]), (corner[2], 1 - corner[2])),
    )


def assemble(positions, cell_valid):
    offsets_list = stencil_offsets()
    full_shape = positions.shape[1:]
    inside = cell_valid[:, :, None]
    entry_sums = {}
    mass_sums = {}
    for corners in kuhn_tetrahedra():
        anchor = corner_slice(positions, corners[0])
        edge_one = corner_slice(positions, corners[1]) - anchor
        edge_two = corner_slice(positions, corners[2]) - anchor
        edge_three = corner_slice(positions, corners[3]) - anchor
        grad_one = jnp.cross(edge_two, edge_three, axis=0)
        grad_two = jnp.cross(edge_three, edge_one, axis=0)
        grad_three = jnp.cross(edge_one, edge_two, axis=0)
        gradients = [-(grad_one + grad_two + grad_three), grad_one, grad_two, grad_three]
        determinant = jnp.sum(edge_one * grad_one, axis=0)
        volume_six = jnp.where(inside, jnp.abs(determinant), 1.0)
        weight = jnp.where(inside, 1.0 / (6.0 * volume_six), 0.0)
        for first in range(4):
            for second in range(4):
                entry_value = jnp.sum(gradients[first] * gradients[second], axis=0) * weight
                shift_key = (
                    corners[second][0] - corners[first][0],
                    corners[second][1] - corners[first][1],
                    corners[second][2] - corners[first][2],
                )
                slot_key = (corners[first], offsets_list.index(shift_key))
                if slot_key in entry_sums:
                    entry_sums[slot_key] = entry_sums[slot_key] + entry_value
                else:
                    entry_sums[slot_key] = entry_value
        portion = jnp.where(inside, volume_six / 24.0, 0.0)
        for corner in corners:
            if corner in mass_sums:
                mass_sums[corner] = mass_sums[corner] + portion
            else:
                mass_sums[corner] = portion
    totals = [jnp.zeros(full_shape, jnp.float32) for entry in offsets_list]
    for slot_key in entry_sums:
        totals[slot_key[1]] = totals[slot_key[1]] + placed_at(entry_sums[slot_key], slot_key[0])
    mass_total = jnp.zeros(full_shape, jnp.float32)
    for corner in mass_sums:
        mass_total = mass_total + placed_at(mass_sums[corner], corner)
    coefs = jnp.stack([entry[1:-1, 1:-1, :] for entry in totals])
    return (coefs, mass_total[1:-1, 1:-1, :])


def window_positions(extended_offsets, index_a, index_b):
    depth = extended_offsets.shape[3]
    grid_a = jnp.broadcast_to(
        index_a.astype(jnp.float32)[:, None, None], extended_offsets.shape[1:]
    )
    grid_b = jnp.broadcast_to(
        index_b.astype(jnp.float32)[None, :, None], extended_offsets.shape[1:]
    )
    grid_c = jnp.broadcast_to(
        jnp.arange(depth, dtype=jnp.int32).astype(jnp.float32)[None, None, :],
        extended_offsets.shape[1:],
    )
    return jnp.stack([grid_a, grid_b, grid_c]) + extended_offsets


def stiffness_apply(extended, coefs):
    offsets_list = stencil_offsets()
    rows_a = extended.shape[1] - 2
    rows_b = extended.shape[2] - 2
    depth = extended.shape[3]
    padded = jnp.pad(extended, ((0, 0), (0, 0), (0, 0), (1, 1)))
    result = jnp.zeros((extended.shape[0], rows_a, rows_b, depth), jnp.float32)
    for position, shift_key in enumerate(offsets_list):
        result = (
            result
            + coefs[position]
            * padded[
                :,
                1 + shift_key[0] : 1 + shift_key[0] + rows_a,
                1 + shift_key[1] : 1 + shift_key[1] + rows_b,
                1 + shift_key[2] : 1 + shift_key[2] + depth,
            ]
        )
    return result


def local_grams(vectors, k_vectors, mass):
    flat = vectors.reshape(vectors.shape[0], -1)
    k_flat = k_vectors.reshape(vectors.shape[0], -1)
    m_flat = flat * mass.reshape(1, -1)
    gram_k = lax.dot_general(
        flat, k_flat, (((1,), (1,)), ((), ())), precision=lax.Precision.HIGHEST
    )
    gram_m = lax.dot_general(
        flat, m_flat, (((1,), (1,)), ((), ())), precision=lax.Precision.HIGHEST
    )
    return (gram_k, gram_m)


def spread_sum(rows):
    plane = ("px", "pc")
    count = lax.axis_size("px") * lax.axis_size("pc")
    depth = lax.axis_size("pz")
    pieces = rows.reshape(count, -1, rows.shape[1])
    part = jnp.sum(lax.all_to_all(pieces, plane, 0, 0), axis=0)
    part = jnp.sum(
        lax.all_to_all(jnp.broadcast_to(part[None], (depth,) + part.shape), "pz", 0, 0), axis=0
    )
    whole = lax.all_to_all(jnp.broadcast_to(part[None], (count,) + part.shape), plane, 0, 0)
    return whole.reshape(rows.shape)


def summed_grams(gram_k, gram_m):
    order = gram_k.shape[0]
    eye = jnp.eye(order, dtype=jnp.bool_)
    square = jnp.triu(gram_k) + jnp.tril(gram_m, -1)
    diagonal = jnp.sum(jnp.where(eye, gram_m, 0.0), axis=0)
    rows = jnp.concatenate([square, jnp.broadcast_to(diagonal[None], (256 - order, order))])
    return spread_sum(jnp.pad(rows, ((0, 0), (0, 256 - order))))


def shards(offsets, block, prior):
    vecs = block.shape[0]
    rows_a = block.shape[1]
    rows_b = block.shape[2]
    depth = block.shape[3]
    total_a = rows_a * lax.axis_size("px")
    total_b = rows_b * lax.axis_size(("pz", "pc"))
    start_a = lax.axis_index("px") * rows_a
    start_b = lax.axis_index(("pz", "pc")) * rows_b
    sides = (("px", 1), (("pz", "pc"), 2))
    wide = padded_2(jnp.concatenate([offsets, block]), sides, 2)
    prior_wide = padded_2(prior, sides, 1)
    extended_offsets = wide[: offsets.shape[0]]
    block_wide = wide[offsets.shape[0] :]
    index_a = start_a - 2 + jnp.arange(rows_a + 4, dtype=jnp.int32)
    index_b = start_b - 2 + jnp.arange(rows_b + 4, dtype=jnp.int32)
    positions = window_positions(extended_offsets, index_a, index_b)
    cells_a = index_a[:-1]
    cells_b = index_b[:-1]
    valid_a = (cells_a >= 0) & (cells_a <= total_a - 2)
    valid_b = (cells_b >= 0) & (cells_b <= total_b - 2)
    coefs_wide, mass_wide = assemble(positions, valid_a[:, None] & valid_b[None, :])
    coefs = coefs_wide[:, 1:-1, 1:-1, :]
    mass = mass_wide[1:-1, 1:-1, :]
    centre = stencil_offsets().index((0, 0, 0))
    vertex_a = index_a[1:-1]
    vertex_b = index_b[1:-1]
    inside_a = (vertex_a >= 0) & (vertex_a <= total_a - 1)
    inside_b = (vertex_b >= 0) & (vertex_b <= total_b - 1)
    inside = (inside_a[:, None] & inside_b[None, :])[:, :, None]
    diagonal = jnp.where(inside, coefs_wide[centre], 1.0)
    k_wide = stiffness_apply(block_wide, coefs_wide)
    u_wide = k_wide / diagonal
    w_wide = mass_wide * block_wide[:, 1:-1, 1:-1, :] / diagonal
    applied = stiffness_apply(jnp.concatenate([u_wide, w_wide, prior_wide]), coefs)
    u_part = u_wide[:, 1:-1, 1:-1, :]
    w_part = w_wide[:, 1:-1, 1:-1, :]
    basis = jnp.concatenate([block, u_part, w_part, prior])
    k_basis = jnp.concatenate([k_wide[:, 1:-1, 1:-1, :], applied])
    coeffs, quotient = ritz_call(summed_grams(*local_grams(basis, k_basis, mass)))
    search = u_part - quotient[:, :1, None, None] * w_part
    scale = jnp.sqrt(jnp.float32(total_a * total_b * depth))
    flat_basis = jnp.concatenate([block, search, prior]).reshape(3 * vecs, -1)
    new_block = scale * lax.dot_general(
        coeffs, flat_basis, (((1,), (0,)), ((), ())), precision=lax.Precision.HIGHEST
    )
    return (new_block.reshape(block.shape), search)


def solution(mesh):
    grid = Mesh(
        mesh.devices.reshape(mesh.shape["px"], mesh.shape["py"] // 2, 2), ("px", "pz", "pc")
    )
    spec = P(None, "px", ("pz", "pc"), None)
    return jax.shard_map(
        shards, mesh=grid, in_specs=(spec, spec, spec), out_specs=(spec, spec), check_vma=False
    )
```

```python
import math

import jax
import jax.numpy as jnp
from jax import lax
from jax.experimental import pallas as pl
from jax.experimental.pallas import tpu as pltpu
from jax.sharding import Mesh
from jax.sharding import PartitionSpec as P

VECS = 48
HI = lax.Precision.HIGHEST
FORWARD = [(0, 0, 1), (0, 1, 0), (0, 1, 1), (1, 0, 0), (1, 0, 1), (1, 1, 0), (1, 1, 1)]
VMEM = pltpu.VMEM


def dots(a, b, dims):
    return lax.dot_general(a, b, (dims, ((), ())), precision=HI, preferred_element_type=jnp.float32)


def eliminated(gram):
    order = gram.shape[0]
    third = order // 3
    rows = lax.broadcasted_iota(jnp.int32, gram.shape, 0)
    cols = lax.broadcasted_iota(jnp.int32, gram.shape, 1)
    inverse = jnp.where(rows == cols, 1.0, 0.0).astype(jnp.float32)
    place = lax.broadcasted_iota(jnp.int32, (third, 128), 0)
    done = []
    for j in range(3):
        left = gram[:third]
        right = inverse[:third]
        gram = gram[third:]
        inverse = inverse[third:]
        pivots = jnp.ones((third, 128), jnp.float32)
        for k in range(third):
            c = third * j + k
            column = jnp.broadcast_to(left[:, c : c + 1], (third, 128))
            pivot = column[k : k + 1, :]
            pivots = jnp.where(place == k, pivot, pivots)
            factor = jnp.where(place > k, column * (1.0 / pivot), 0.0)
            factor = jnp.concatenate([factor, factor], axis=1)
            left, right = (
                left - factor * left[k : k + 1, :],
                right - factor * right[k : k + 1, :],
            )
        scale = 1.0 / jnp.sqrt(pivots)
        scale = jnp.concatenate([scale, scale], axis=1)
        left = left * scale
        right = right * scale
        done.append(right)
        if j < 2:
            flipped = left.T[third * (j + 1) : order]
            gram = gram - dots(flipped, left, ((1,), (0,)))
            inverse = inverse - dots(flipped, right, ((1,), (0,)))
    return jnp.concatenate(done, axis=0)


def ritz_core(total):
    vecs = VECS
    order = 3 * vecs
    full = 4 * vecs
    rows = lax.broadcasted_iota(jnp.int32, total.shape, 0)
    cols = lax.broadcasted_iota(jnp.int32, total.shape, 1)
    flipped = total.T
    diagonal = total[full : full + 1, :]
    gram_k = jnp.where(rows <= cols, total, flipped)
    gram_m = jnp.where(rows > cols, total, jnp.where(rows == cols, diagonal, flipped))
    eye = rows == cols
    top = lambda g: jnp.sum(jnp.where(eye, g, 0.0)[:vecs], axis=1, keepdims=True)
    quotient = top(gram_k) / top(gram_m)

    def joined(g):
        mid = g[vecs : 2 * vecs] - quotient * g[2 * vecs : 3 * vecs]
        return jnp.concatenate([g[:vecs], mid, g[3 * vecs : full]], axis=0)

    gram_k = joined(joined(gram_k).T)
    gram_m = joined(joined(gram_m).T)
    gram_m = jnp.concatenate([gram_m, jnp.zeros((order, 256 - order), jnp.float32)], axis=1)
    inverse = eliminated(gram_m)[:, :order]
    half = dots(inverse, gram_k, ((1,), (0,)))
    reduced = dots(half, inverse, ((1,), (1,)))
    bound = jnp.max(jnp.sum(jnp.abs(reduced), axis=1, keepdims=True), axis=0, keepdims=True)
    eye = lax.broadcasted_iota(jnp.int32, (order, order), 0) == lax.broadcasted_iota(
        jnp.int32, (order, order), 1
    )
    shifted = jnp.where(eye, 1.0, 0.0) - reduced / bound
    filtered = dots(shifted[:vecs], shifted, ((1,), (0,)))
    return dots(filtered, inverse, ((1,), (0,))), quotient


def kuhn_tetrahedra():
    orders = [(0, 1, 2), (0, 2, 1), (1, 0, 2), (1, 2, 0), (2, 0, 1), (2, 1, 0)]
    tetrahedra = []
    for ordering in orders:
        corner = [0, 0, 0]
        corners = [(0, 0, 0)]
        for axis_step in ordering:
            corner[axis_step] = 1
            corners.append((corner[0], corner[1], corner[2]))
        tetrahedra.append(corners)
    return tetrahedra


def cross(p, q):
    return (
        p[1] * q[2] - p[2] * q[1],
        p[2] * q[0] - p[0] * q[2],
        p[0] * q[1] - p[1] * q[0],
    )


def dot3(p, q):
    return p[0] * q[0] + p[1] * q[1] + p[2] * q[2]


def shifted_lanes(x, step):
    return pltpu.roll(x, (-step) % x.shape[-1], x.ndim - 1)


def shifted_rows(x, step):
    return pltpu.roll(x, (-step) % x.shape[-2], x.ndim - 2)


def assemble_tables(off_ref, coef_ref, start_a, start_b, total_a, total_b):
    shape = (16, 128)
    row = lax.broadcasted_iota(jnp.int32, shape, 0)
    lane = lax.broadcasted_iota(jnp.int32, shape, 1)
    grid_b = start_b - 2 + row
    valid_bc = (grid_b >= 0) & (grid_b <= total_b - 2) & (row < 11) & (lane < 127)
    coef_ref[...] = jnp.zeros(coef_ref.shape, jnp.float32)

    def plane(a):
        grid_a = (start_a - 2 + a).astype(jnp.float32)
        base = [
            off_ref[0, a] + grid_a,
            off_ref[1, a] + grid_b.astype(jnp.float32),
            off_ref[2, a] + lane.astype(jnp.float32),
        ]
        out = {}
        for db in (0, 1):
            moved = [shifted_rows(p, db) if db else p for p in base]
            for dc in (0, 1):
                out[(db, dc)] = [shifted_lanes(p, dc) if dc else p for p in moved]
        return out

    def add(slot, a, value, b_shift, c_shift):
        if c_shift:
            value = shifted_lanes(value, -1)
        if b_shift == 0:
            value = shifted_rows(value, 1)
        coef_ref[slot, a] = coef_ref[slot, a] + value

    low = plane(0)
    for a in range(7):
        high = plane(a + 1)
        at = lambda corner: (high if corner[0] else low)[(corner[1], corner[2])]
        cell_a = start_a - 2 + a
        inside = valid_bc & (cell_a >= 0) & (cell_a <= total_a - 2)
        sums = {}
        for corners in kuhn_tetrahedra():
            anchor = at(corners[0])
            edges = [tuple(x - y for x, y in zip(at(c), anchor)) for c in corners[1:]]
            g1 = cross(edges[1], edges[2])
            g2 = cross(edges[2], edges[0])
            g3 = cross(edges[0], edges[1])
            g0 = tuple(-(x + y + z) for x, y, z in zip(g1, g2, g3))
            grads = [g0, g1, g2, g3]
            det = jnp.where(inside, jnp.abs(dot3(edges[0], g1)), 1.0)
            weight = jnp.where(inside, 1.0 / (6.0 * det), 0.0)
            for i in range(4):
                for j in range(i, 4):
                    step = tuple(q - p for p, q in zip(corners[i], corners[j]))
                    slot = 7 if i == j else FORWARD.index(step)
                    key = (slot, corners[i])
                    value = dot3(grads[i], grads[j]) * weight
                    sums[key] = sums[key] + value if key in sums else value
            part = jnp.where(inside, det * (1.0 / 24.0), 0.0)
            for corner in corners:
                key = (8, corner)
                sums[key] = sums[key] + part if key in sums else part
        for (slot, corner), value in sums.items():
            table_a = a + corner[0] - 1
            if 0 <= table_a <= 5:
                add(slot, table_a, value, corner[1], corner[2])
        low = high


def gram_kernel(start_ref, own_ref, down_a, up_a, down_b, up_b, c_pp, c_mm, c_pm, c_mp, off_own,
                gram_ref, uw_ref, off_ref, coef_ref, turn_ref, xb_ref, y_ref, acc_ref):
    v = VECS
    for i in range(3):
        for a in range(4):
            off_ref[i, 2 + a, 2:10] = off_own[i, a]
            off_ref[i, 2 + a, 10:12] = down_b[12, i * 8 + a * 2 : i * 8 + a * 2 + 2]
            off_ref[i, 2 + a, 0:2] = up_b[4, i * 8 + a * 2 : i * 8 + a * 2 + 2]
        for a in range(2):
            off_ref[i, 6 + a, 2:10] = down_a[24, i * 16 + a * 8 : i * 16 + a * 8 + 8]
            off_ref[i, a, 2:10] = up_a[8, i * 16 + a * 8 : i * 16 + a * 8 + 8]
            pair = slice(i * 4 + a * 2, i * 4 + a * 2 + 2)
            off_ref[i, 6 + a, 10:12] = c_pp[5, pair]
            off_ref[i, a, 0:2] = c_mm[1, pair]
            off_ref[i, 6 + a, 0:2] = c_pm[1, pair]
            off_ref[i, a, 10:12] = c_mp[1, pair]
    assemble_tables(off_ref, coef_ref, start_ref[0], start_ref[1], start_ref[2], start_ref[3])
    for slot, (da, db, dc) in enumerate(FORWARD):
        if dc:
            for a in range(6):
                turn_ref[slot, a] = shifted_lanes(coef_ref[slot, a], -1)

    def put(a, b, ref, i):
        xb_ref[a + 1, b + 1] = ref[i]

    for a in range(4):
        for b in range(8):
            xb_ref[a + 1, b + 1] = own_ref[a * 8 + b, :v]
            y_ref[a * 9 + b, 2 * v :] = own_ref[a * 8 + b, v:]
    for b in range(8):
        put(4, b, down_a, b)
        put(5, b, down_a, 8 + b)
        y_ref[4 * 9 + b, 2 * v :] = down_a[16 + b]
        put(-1, b, up_a, b)
    for a in range(4):
        put(a, 8, down_b, a * 2)
        put(a, 9, down_b, a * 2 + 1)
        y_ref[a * 9 + 8, 2 * v :] = down_b[8 + a]
        put(a, -1, up_b, a)
    for a in range(2):
        for b in range(2):
            put(4 + a, 8 + b, c_pp, a * 2 + b)
    y_ref[4 * 9 + 8, 2 * v :] = c_pp[4]
    put(-1, -1, c_mm, 0)
    put(4, -1, c_pm, 0)
    put(-1, 8, c_mp, 0)

    def row(ref, slot, a, b):
        return ref[slot, a, pl.ds(b, 1), :]

    def k_block(a, b):
        x = lambda i, j: xb_ref[a + 1 + i, b + 1 + j]
        total = x(0, 0) * row(coef_ref, 7, a + 1, b + 1)
        ahead = None
        behind = None
        for slot, (da, db, dc) in enumerate(FORWARD):
            front = x(da, db) * row(turn_ref if dc else coef_ref, slot, a + 1, b + 1)
            back = x(-da, -db) * row(coef_ref, slot, a + 1 - da, b + 1 - db)
            if dc:
                ahead = front if ahead is None else ahead + front
                behind = back if behind is None else behind + back
            else:
                total = total + front + back
        return total + shifted_lanes(ahead, 1) + shifted_lanes(behind, -1)

    def first(t, carry):
        a = t // 9
        b = t - a * 9
        kb = k_block(a, b)
        diagonal = row(coef_ref, 7, a + 1, b + 1)
        inverse = 1.0 / jnp.where(diagonal == 0.0, 1.0, diagonal)
        y_ref[t, :v] = kb * inverse
        y_ref[t, v : 2 * v] = xb_ref[a + 1, b + 1] * (row(coef_ref, 8, a + 1, b + 1) * inverse)
        return carry

    lax.fori_loop(0, 45, first, 0)

    acc_ref[...] = jnp.zeros(acc_ref.shape, jnp.float32)

    def sides(a, b):
        t = a * 9 + b
        block = xb_ref[a + 1, b + 1]
        y = y_ref[t]
        diagonal = row(coef_ref, 7, a + 1, b + 1)
        mass = row(coef_ref, 8, a + 1, b + 1)
        straight = y * (0.5 * diagonal)
        ahead = None
        for slot, (da, db, dc) in enumerate(FORWARD):
            front = y_ref[t + 9 * da + db] * row(turn_ref if dc else coef_ref, slot, a + 1, b + 1)
            if dc:
                ahead = front if ahead is None else ahead + front
            else:
                straight = straight + front
        ky = straight + shifted_lanes(ahead, 1)
        kb = y[:v] * diagonal
        basis = jnp.concatenate([block, y], axis=0)
        return basis, jnp.concatenate([kb, ky, basis * mass], axis=0)

    def second(t, carry):
        a = t // 4
        b = (t - a * 4) * 2
        x0, r0 = sides(a, b)
        x1, r1 = sides(a, b + 1)
        uw_ref[a * 8 + b] = x0[v : 3 * v]
        uw_ref[a * 8 + b + 1] = x1[v : 3 * v]
        left = jnp.concatenate([r0, r1], axis=1)
        right = jnp.concatenate([x0, x1], axis=1)
        acc_ref[...] += lax.dot_general(
            left, right, (((1,), (1,)), ((), ())), precision=HI,
            preferred_element_type=jnp.float32)
        return carry

    lax.fori_loop(0, 16, second, 0)

    n = 4 * v
    acc = acc_ref[...]
    pad = lambda g: jnp.concatenate(
        [jnp.concatenate([g, jnp.zeros((n, 256 - n), jnp.float32)], axis=1),
         jnp.zeros((256 - n, 256), jnp.float32)], axis=0)
    half = pad(acc[:n])
    gram_m = pad(acc[n:])
    rows = lax.broadcasted_iota(jnp.int32, (256, 256), 0)
    cols = lax.broadcasted_iota(jnp.int32, (256, 256), 1)
    gram_k = jnp.where(rows < v, half, half + half.T)
    diagonal = jnp.sum(jnp.where(rows == cols, gram_m, 0.0), axis=0, keepdims=True)
    square = jnp.where(rows <= cols, gram_k, gram_m)
    gram_ref[...] = jnp.where(rows < n, square, diagonal)


def gram_call(start, own, pieces, off):
    v = VECS
    spec = pl.BlockSpec(memory_space=VMEM)
    return pl.pallas_call(
        gram_kernel,
        out_shape=(
            jax.ShapeDtypeStruct((256, 256), jnp.float32),
            jax.ShapeDtypeStruct((32, 2 * v, 128), jnp.float32),
        ),
        in_specs=[pl.BlockSpec(memory_space=pltpu.SMEM)] + [spec] * (2 + len(pieces)),
        out_specs=(spec, spec),
        scratch_shapes=[
            VMEM((3, 8, 16, 128), jnp.float32),
            VMEM((9, 6, 16, 128), jnp.float32),
            VMEM((7, 6, 16, 128), jnp.float32),
            VMEM((7, 11, v, 128), jnp.float32),
            VMEM((45, 3 * v, 128), jnp.float32),
            VMEM((8 * v, 4 * v), jnp.float32),
        ],
        compiler_params=pltpu.CompilerParams(vmem_limit_bytes=48 * 2**20),
    )(start, own, *pieces, off)


def finish_kernel(scale, total_ref, own_hbm, uw_hbm, new_ref, search_ref, own_ref, uw_ref, sems):
    v = VECS
    copies = [
        pltpu.make_async_copy(own_hbm, own_ref, sems.at[0]),
        pltpu.make_async_copy(uw_hbm, uw_ref, sems.at[1]),
    ]
    for copy in copies:
        copy.start()
    coeffs, quotient = ritz_core(total_ref[...])
    coeffs = coeffs * scale
    quotient = jnp.broadcast_to(quotient, (v, 128))
    for copy in copies:
        copy.wait()
    for t in range(0, 32, 2):
        basis = []
        for i in (t, t + 1):
            search = uw_ref[i, :v] - quotient * uw_ref[i, v:]
            search_ref[pl.ds(i, v, stride=32), :] = search
            basis.append(jnp.concatenate([own_ref[i, :v], search, own_ref[i, v:]], axis=0))
        new = dots(coeffs, jnp.concatenate(basis, axis=1), ((1,), (0,)))
        new_ref[pl.ds(t, v, stride=32), :] = new[:, :128]
        new_ref[pl.ds(t + 1, v, stride=32), :] = new[:, 128:]


def finish_call(scale, total, own, uw):
    v = VECS
    vmem = pl.BlockSpec(memory_space=VMEM)
    hbm = pl.BlockSpec(memory_space=pl.ANY)
    out = jax.ShapeDtypeStruct((v * 32, 128), jnp.float32)
    return pl.pallas_call(
        lambda *refs: finish_kernel(scale, *refs),
        out_shape=(out, out),
        in_specs=[vmem, hbm, hbm],
        out_specs=(vmem, vmem),
        scratch_shapes=[
            VMEM((32, 2 * v, 128), jnp.float32),
            VMEM((32, 2 * v, 128), jnp.float32),
            pltpu.SemaphoreType.DMA((2,)),
        ],
        compiler_params=pltpu.CompilerParams(vmem_limit_bytes=48 * 2**20),
    )(total, own, uw)


def spread_sum(rows):
    plane = ("px", "pc")
    count = lax.axis_size("px") * lax.axis_size("pc")
    depth = lax.axis_size("pz")
    pieces = rows.reshape(count, -1, rows.shape[1])
    part = jnp.sum(lax.all_to_all(pieces, plane, 0, 0), axis=0)
    part = jnp.sum(
        lax.all_to_all(jnp.broadcast_to(part[None], (depth,) + part.shape), "pz", 0, 0), axis=0
    )
    whole = lax.all_to_all(jnp.broadcast_to(part[None], (count,) + part.shape), plane, 0, 0)
    return whole.reshape(rows.shape)


def neighbour(payload, step_a, step_b):
    count_a = lax.axis_size("px")
    count_b = lax.axis_size("pz") * lax.axis_size("pc")
    pairs = []
    for a in range(count_a):
        for b in range(count_b):
            if 0 <= a + step_a < count_a and 0 <= b + step_b < count_b:
                pairs.append(((a + step_a) * count_b + b + step_b, a * count_b + b))
    return lax.ppermute(payload, ("px", "pz", "pc"), pairs)


def shards(offsets, block, prior):
    v = block.shape[0]
    rows_a, rows_b, depth = block.shape[1:]
    total_a = rows_a * lax.axis_size("px")
    total_b = rows_b * lax.axis_size("pz") * lax.axis_size("pc")
    start = jnp.stack(
        [
            lax.axis_index("px") * rows_a,
            lax.axis_index(("pz", "pc")) * rows_b,
            jnp.int32(total_a),
            jnp.int32(total_b),
        ]
    ).astype(jnp.int32)
    own = jnp.concatenate([block, prior]).transpose(1, 2, 0, 3)

    def payload(b_a, b_b, p_a, p_b, o_a, o_b):
        parts = [own[b_a, b_b, :v].reshape(-1, v, depth)]
        if p_a is not None:
            parts.append(own[p_a, p_b, v:].reshape(-1, v, depth))
        rows = offsets[:, o_a, o_b].reshape(-1, depth)
        parts.append(jnp.pad(rows, ((0, v - rows.shape[0]), (0, 0)))[None])
        return jnp.concatenate(parts)

    low, high, every = slice(0, 2), slice(-2, None), slice(None)
    first, last = slice(0, 1), slice(-1, None)
    down_a = neighbour(payload(low, every, first, every, low, every), 1, 0)
    up_a = neighbour(payload(last, every, None, None, high, every), -1, 0)
    down_b = neighbour(payload(every, low, every, first, every, low), 0, 1)
    up_b = neighbour(payload(every, last, None, None, every, high), 0, -1)
    c_pp = neighbour(payload(low, low, first, first, low, low), 1, 1)
    c_mm = neighbour(payload(last, last, None, None, high, high), -1, -1)
    c_pm = neighbour(payload(first, last, None, None, low, high), 1, -1)
    c_mp = neighbour(payload(last, first, None, None, high, low), -1, 1)
    own = own.reshape(rows_a * rows_b, 2 * v, depth)
    pieces = (down_a, up_a, down_b, up_b, c_pp, c_mm, c_pm, c_mp)
    gram, uw = gram_call(start, own, pieces, offsets)
    scale = math.sqrt(total_a * total_b * depth)
    new_block, search = finish_call(scale, spread_sum(gram), own, uw)
    return (new_block.reshape(block.shape), search.reshape(block.shape))


def solution(mesh):
    grid = Mesh(
        mesh.devices.reshape(mesh.shape["px"], mesh.shape["py"] // 2, 2), ("px", "pz", "pc")
    )
    spec = P(None, "px", ("pz", "pc"), None)
    return jax.shard_map(
        shards, mesh=grid, in_specs=(spec, spec, spec), out_specs=(spec, spec), check_vma=False
    )
```

```python
import math

import jax
import jax.numpy as jnp
from jax import lax
from jax.experimental import pallas as pl
from jax.experimental.pallas import tpu as pltpu
from jax.sharding import Mesh
from jax.sharding import PartitionSpec as P

VECS = 48
HI = lax.Precision.HIGHEST
FORWARD = [(0, 0, 1), (0, 1, 0), (0, 1, 1), (1, 0, 0), (1, 0, 1), (1, 1, 0), (1, 1, 1)]
VMEM = pltpu.VMEM


def dots(a, b, dims):
    return lax.dot_general(a, b, (dims, ((), ())), precision=HI, preferred_element_type=jnp.float32)


def eliminated(gram):
    order = gram.shape[0]
    third = order // 3
    rows = lax.broadcasted_iota(jnp.int32, gram.shape, 0)
    cols = lax.broadcasted_iota(jnp.int32, gram.shape, 1)
    inverse = jnp.where(rows == cols, 1.0, 0.0).astype(jnp.float32)
    place = lax.broadcasted_iota(jnp.int32, (third, 128), 0)
    done = []
    for j in range(3):
        left = gram[:third]
        right = inverse[:third]
        gram = gram[third:]
        inverse = inverse[third:]
        pivots = jnp.ones((third, 128), jnp.float32)
        for k in range(third):
            c = third * j + k
            column = jnp.broadcast_to(left[:, c : c + 1], (third, 128))
            pivot = column[k : k + 1, :]
            pivots = jnp.where(place == k, pivot, pivots)
            factor = jnp.where(place > k, column * (1.0 / pivot), 0.0)
            factor = jnp.concatenate([factor, factor], axis=1)
            left, right = (
                left - factor * left[k : k + 1, :],
                right - factor * right[k : k + 1, :],
            )
        scale = 1.0 / jnp.sqrt(pivots)
        scale = jnp.concatenate([scale, scale], axis=1)
        left = left * scale
        right = right * scale
        done.append(right)
        if j < 2:
            flipped = left.T[third * (j + 1) : order]
            gram = gram - dots(flipped, left, ((1,), (0,)))
            inverse = inverse - dots(flipped, right, ((1,), (0,)))
    return jnp.concatenate(done, axis=0)


def ritz_core(total):
    vecs = VECS
    order = 3 * vecs
    full = 4 * vecs
    rows = lax.broadcasted_iota(jnp.int32, total.shape, 0)
    cols = lax.broadcasted_iota(jnp.int32, total.shape, 1)
    flipped = total.T
    diagonal = total[full : full + 1, :]
    gram_k = jnp.where(rows <= cols, total, flipped)
    gram_m = jnp.where(rows > cols, total, jnp.where(rows == cols, diagonal, flipped))
    eye = rows == cols
    top = lambda g: jnp.sum(jnp.where(eye, g, 0.0)[:vecs], axis=1, keepdims=True)
    quotient = top(gram_k) / top(gram_m)

    def joined(g):
        mid = g[vecs : 2 * vecs] - quotient * g[2 * vecs : 3 * vecs]
        return jnp.concatenate([g[:vecs], mid, g[3 * vecs : full]], axis=0)

    gram_k = joined(joined(gram_k).T)
    gram_m = joined(joined(gram_m).T)
    gram_m = jnp.concatenate([gram_m, jnp.zeros((order, 256 - order), jnp.float32)], axis=1)
    inverse = eliminated(gram_m)[:, :order]
    half = dots(inverse, gram_k, ((1,), (0,)))
    reduced = dots(half, inverse, ((1,), (1,)))
    bound = jnp.max(jnp.sum(jnp.abs(reduced), axis=1, keepdims=True), axis=0, keepdims=True)
    eye = lax.broadcasted_iota(jnp.int32, (order, order), 0) == lax.broadcasted_iota(
        jnp.int32, (order, order), 1
    )
    shifted = jnp.where(eye, 1.0, 0.0) - reduced / bound
    filtered = dots(shifted[:vecs], shifted, ((1,), (0,)))
    return dots(filtered, inverse, ((1,), (0,))), quotient


def kuhn_tetrahedra():
    orders = [(0, 1, 2), (0, 2, 1), (1, 0, 2), (1, 2, 0), (2, 0, 1), (2, 1, 0)]
    tetrahedra = []
    for ordering in orders:
        corner = [0, 0, 0]
        corners = [(0, 0, 0)]
        for axis_step in ordering:
            corner[axis_step] = 1
            corners.append((corner[0], corner[1], corner[2]))
        tetrahedra.append(corners)
    return tetrahedra


def cross(p, q):
    return (
        p[1] * q[2] - p[2] * q[1],
        p[2] * q[0] - p[0] * q[2],
        p[0] * q[1] - p[1] * q[0],
    )


def dot3(p, q):
    return p[0] * q[0] + p[1] * q[1] + p[2] * q[2]


def shifted_lanes(x, step):
    return pltpu.roll(x, (-step) % x.shape[-1], x.ndim - 1)


def shifted_rows(x, step):
    return pltpu.roll(x, (-step) % x.shape[-2], x.ndim - 2)


def assemble_tables(off_ref, coef_ref, start_a, start_b, total_a, total_b):
    shape = (16, 128)
    row = lax.broadcasted_iota(jnp.int32, shape, 0)
    lane = lax.broadcasted_iota(jnp.int32, shape, 1)
    grid_b = start_b - 2 + row
    valid_bc = (grid_b >= 0) & (grid_b <= total_b - 2) & (row < 11) & (lane < 127)
    coef_ref[...] = jnp.zeros(coef_ref.shape, jnp.float32)

    def plane(a):
        grid_a = (start_a - 2 + a).astype(jnp.float32)
        base = [
            off_ref[0, a] + grid_a,
            off_ref[1, a] + grid_b.astype(jnp.float32),
            off_ref[2, a] + lane.astype(jnp.float32),
        ]
        out = {}
        for db in (0, 1):
            moved = [shifted_rows(p, db) if db else p for p in base]
            for dc in (0, 1):
                out[(db, dc)] = [shifted_lanes(p, dc) if dc else p for p in moved]
        return out

    def add(slot, a, value, b_shift, c_shift):
        if c_shift:
            value = shifted_lanes(value, -1)
        if b_shift == 0:
            value = shifted_rows(value, 1)
        coef_ref[slot, a] = coef_ref[slot, a] + value

    low = plane(0)
    for a in range(7):
        high = plane(a + 1)
        at = lambda corner: (high if corner[0] else low)[(corner[1], corner[2])]
        cell_a = start_a - 2 + a
        inside = valid_bc & (cell_a >= 0) & (cell_a <= total_a - 2)
        sums = {}
        for corners in kuhn_tetrahedra():
            anchor = at(corners[0])
            edges = [tuple(x - y for x, y in zip(at(c), anchor)) for c in corners[1:]]
            g1 = cross(edges[1], edges[2])
            g2 = cross(edges[2], edges[0])
            g3 = cross(edges[0], edges[1])
            g0 = tuple(-(x + y + z) for x, y, z in zip(g1, g2, g3))
            grads = [g0, g1, g2, g3]
            det = jnp.where(inside, jnp.abs(dot3(edges[0], g1)), 1.0)
            weight = jnp.where(inside, 1.0 / (6.0 * det), 0.0)
            for i in range(4):
                for j in range(i, 4):
                    step = tuple(q - p for p, q in zip(corners[i], corners[j]))
                    slot = 7 if i == j else FORWARD.index(step)
                    key = (slot, corners[i])
                    value = dot3(grads[i], grads[j]) * weight
                    sums[key] = sums[key] + value if key in sums else value
            part = jnp.where(inside, det * (1.0 / 24.0), 0.0)
            for corner in corners:
                key = (8, corner)
                sums[key] = sums[key] + part if key in sums else part
        for (slot, corner), value in sums.items():
            table_a = a + corner[0] - 1
            if 0 <= table_a <= 5:
                add(slot, table_a, value, corner[1], corner[2])
        low = high


def pack_kernel(block_ref, prior_ref, off_ref, own, down_a, up_a, down_b, up_b, c_pp, c_mm, c_pm, c_mp):
    v = VECS
    block = lambda a, b: block_ref[pl.ds(a * 8 + b, v, stride=32), :]
    prior = lambda a, b: prior_ref[pl.ds(a * 8 + b, v, stride=32), :]
    for a in range(4):
        for b in range(8):
            x = block(a, b)
            y = prior(a, b)
            own[a, b, :v] = x
            own[a, b, v:] = y
            if a < 2:
                down_a[a * 8 + b] = x
            if a == 0:
                down_a[16 + b] = y
            if a == 3:
                up_a[b] = x
            if b < 2:
                down_b[b * 4 + a] = x
            if b == 0:
                down_b[8 + a] = y
            if b == 7:
                up_b[a] = x
            if a < 2 and b < 2:
                c_pp[a * 2 + b] = x
            if a == 0 and b == 0:
                c_pp[4] = y
            if a == 3 and b == 7:
                c_mm[0] = x
            if a == 0 and b == 7:
                c_pm[0] = x
            if a == 3 and b == 0:
                c_mp[0] = x
    for i in range(3):
        for a in range(4):
            down_b[12, i * 8 + a * 2 : i * 8 + a * 2 + 2] = off_ref[i, a, 0:2]
            up_b[4, i * 8 + a * 2 : i * 8 + a * 2 + 2] = off_ref[i, a, 6:8]
        for a in range(2):
            down_a[24, i * 16 + a * 8 : i * 16 + a * 8 + 8] = off_ref[i, a]
            up_a[8, i * 16 + a * 8 : i * 16 + a * 8 + 8] = off_ref[i, 2 + a]
            pair = slice(i * 4 + a * 2, i * 4 + a * 2 + 2)
            c_pp[5, pair] = off_ref[i, a, 0:2]
            c_mm[1, pair] = off_ref[i, 2 + a, 6:8]
            c_pm[1, pair] = off_ref[i, a, 6:8]
            c_mp[1, pair] = off_ref[i, 2 + a, 0:2]


def pack_call(block, prior, offsets):
    v = VECS
    vmem = pl.BlockSpec(memory_space=VMEM)
    sizes = [(4, 8, 2 * v, 128)] + [(n, v, 128) for n in (25, 9, 13, 5, 6, 2, 2, 2)]
    return pl.pallas_call(
        pack_kernel,
        out_shape=tuple(jax.ShapeDtypeStruct(s, jnp.float32) for s in sizes),
        in_specs=[vmem] * 3,
        out_specs=(vmem,) * len(sizes),
        compiler_params=pltpu.CompilerParams(vmem_limit_bytes=60 * 2**20),
    )(block.reshape(-1, 128), prior.reshape(-1, 128), offsets)


def gram_kernel(start_ref, own, down_a, up_a, down_b, up_b, c_pp, c_mm, c_pm, c_mp, off_own,
                gram_ref, uw_ref, edge_ref, off_ref, coef_ref, turn_ref, xb_ref, y_ref, acc_ref,
                sems):
    v = VECS
    moves = [
        (piece.at[piece.shape[0] - 1], edge_ref.at[i])
        for i, piece in enumerate((down_a, up_a, down_b, up_b, c_pp, c_mm, c_pm, c_mp))
    ]
    third = slice(2 * v, 3 * v)
    moves += [
        (own.at[:, :, :v], xb_ref.at[1:5, 1:9]),
        (down_a.at[0:8], xb_ref.at[5, 1:9]),
        (down_a.at[8:16], xb_ref.at[6, 1:9]),
        (up_a.at[0:8], xb_ref.at[0, 1:9]),
        (down_b.at[0:4], xb_ref.at[1:5, 9]),
        (down_b.at[4:8], xb_ref.at[1:5, 10]),
        (up_b.at[0:4], xb_ref.at[1:5, 0]),
        (c_pp.at[0:2], xb_ref.at[5, 9:11]),
        (c_pp.at[2:4], xb_ref.at[6, 9:11]),
        (c_mm.at[0], xb_ref.at[0, 0]),
        (c_pm.at[0], xb_ref.at[5, 0]),
        (c_mp.at[0], xb_ref.at[0, 9]),
        (own.at[:, :, v:], y_ref.at[0:4, 0:8, third]),
        (down_a.at[16:24], y_ref.at[4, 0:8, third]),
        (down_b.at[8:12], y_ref.at[0:4, 8, third]),
        (c_pp.at[4], y_ref.at[4, 8, third]),
    ]
    copies = [pltpu.make_async_copy(x, y, sems.at[i]) for i, (x, y) in enumerate(moves)]
    for copy in copies:
        copy.start()
    for copy in copies[:8]:
        copy.wait()
    for i in range(3):
        for a in range(4):
            off_ref[i, 2 + a, 2:10] = off_own[i, a]
            pair = slice(i * 8 + a * 2, i * 8 + a * 2 + 2)
            off_ref[i, 2 + a, 10:12] = edge_ref[2, pair]
            off_ref[i, 2 + a, 0:2] = edge_ref[3, pair]
        for a in range(2):
            rows = slice(i * 16 + a * 8, i * 16 + a * 8 + 8)
            off_ref[i, 6 + a, 2:10] = edge_ref[0, rows]
            off_ref[i, a, 2:10] = edge_ref[1, rows]
            pair = slice(i * 4 + a * 2, i * 4 + a * 2 + 2)
            off_ref[i, 6 + a, 10:12] = edge_ref[4, pair]
            off_ref[i, a, 0:2] = edge_ref[5, pair]
            off_ref[i, 6 + a, 0:2] = edge_ref[6, pair]
            off_ref[i, a, 10:12] = edge_ref[7, pair]
    assemble_tables(off_ref, coef_ref, start_ref[0], start_ref[1], start_ref[2], start_ref[3])
    for slot, (da, db, dc) in enumerate(FORWARD):
        if dc:
            for a in range(6):
                turn_ref[slot, a] = shifted_lanes(coef_ref[slot, a], -1)
    for copy in copies[8:]:
        copy.wait()

    def row(ref, slot, a, b):
        return ref[slot, a, pl.ds(b, 1), :]

    def k_block(a, b):
        x = lambda i, j: xb_ref[a + 1 + i, b + 1 + j]
        total = x(0, 0) * row(coef_ref, 7, a + 1, b + 1)
        ahead = None
        behind = None
        for slot, (da, db, dc) in enumerate(FORWARD):
            front = x(da, db) * row(turn_ref if dc else coef_ref, slot, a + 1, b + 1)
            back = x(-da, -db) * row(coef_ref, slot, a + 1 - da, b + 1 - db)
            if dc:
                ahead = front if ahead is None else ahead + front
                behind = back if behind is None else behind + back
            else:
                total = total + front + back
        return total + shifted_lanes(ahead, 1) + shifted_lanes(behind, -1)

    def first(t, carry):
        a = t // 9
        b = t - a * 9
        kb = k_block(a, b)
        diagonal = row(coef_ref, 7, a + 1, b + 1)
        inverse = 1.0 / jnp.where(diagonal == 0.0, 1.0, diagonal)
        y_ref[a, b, :v] = kb * inverse
        y_ref[a, b, v : 2 * v] = xb_ref[a + 1, b + 1] * (row(coef_ref, 8, a + 1, b + 1) * inverse)
        return carry

    lax.fori_loop(0, 45, first, 0)

    acc_ref[...] = jnp.zeros(acc_ref.shape, jnp.float32)

    def sides(a, b):
        block = xb_ref[a + 1, b + 1]
        y = y_ref[a, b]
        diagonal = row(coef_ref, 7, a + 1, b + 1)
        mass = row(coef_ref, 8, a + 1, b + 1)
        straight = y * (0.5 * diagonal)
        ahead = None
        for slot, (da, db, dc) in enumerate(FORWARD):
            front = y_ref[a + da, b + db] * row(turn_ref if dc else coef_ref, slot, a + 1, b + 1)
            if dc:
                ahead = front if ahead is None else ahead + front
            else:
                straight = straight + front
        ky = straight + shifted_lanes(ahead, 1)
        kb = y[:v] * diagonal
        basis = jnp.concatenate([block, y], axis=0)
        return basis, jnp.concatenate([kb, ky, basis * mass], axis=0)

    def second(t, carry):
        a = t // 4
        b = (t - a * 4) * 2
        x0, r0 = sides(a, b)
        x1, r1 = sides(a, b + 1)
        uw_ref[a * 8 + b] = x0[v : 3 * v]
        uw_ref[a * 8 + b + 1] = x1[v : 3 * v]
        left = jnp.concatenate([r0, r1], axis=1)
        right = jnp.concatenate([x0, x1], axis=1)
        acc_ref[...] += lax.dot_general(
            left, right, (((1,), (1,)), ((), ())), precision=HI,
            preferred_element_type=jnp.float32)
        return carry

    lax.fori_loop(0, 16, second, 0)

    n = 4 * v
    acc = acc_ref[...]
    pad = lambda g: jnp.concatenate(
        [jnp.concatenate([g, jnp.zeros((n, 256 - n), jnp.float32)], axis=1),
         jnp.zeros((256 - n, 256), jnp.float32)], axis=0)
    half = pad(acc[:n])
    gram_m = pad(acc[n:])
    rows = lax.broadcasted_iota(jnp.int32, (256, 256), 0)
    cols = lax.broadcasted_iota(jnp.int32, (256, 256), 1)
    gram_k = jnp.where(rows < v, half, half + half.T)
    diagonal = jnp.sum(jnp.where(rows == cols, gram_m, 0.0), axis=0, keepdims=True)
    square = jnp.where(rows <= cols, gram_k, gram_m)
    gram_ref[...] = jnp.where(rows < n, square, diagonal)


def gram_call(start, own, pieces, off):
    v = VECS
    spec = pl.BlockSpec(memory_space=VMEM)
    return pl.pallas_call(
        gram_kernel,
        out_shape=(
            jax.ShapeDtypeStruct((256, 256), jnp.float32),
            jax.ShapeDtypeStruct((32, 2 * v, 128), jnp.float32),
        ),
        in_specs=[pl.BlockSpec(memory_space=pltpu.SMEM)]
        + [pl.BlockSpec(memory_space=pl.ANY)] * (1 + len(pieces))
        + [spec],
        out_specs=(spec, spec),
        scratch_shapes=[
            VMEM((8, v, 128), jnp.float32),
            VMEM((3, 8, 16, 128), jnp.float32),
            VMEM((9, 6, 16, 128), jnp.float32),
            VMEM((7, 6, 16, 128), jnp.float32),
            VMEM((7, 11, v, 128), jnp.float32),
            VMEM((5, 9, 3 * v, 128), jnp.float32),
            VMEM((8 * v, 4 * v), jnp.float32),
            pltpu.SemaphoreType.DMA((24,)),
        ],
        compiler_params=pltpu.CompilerParams(vmem_limit_bytes=12 * 2**20),
    )(start, own, *pieces, off)


def finish_kernel(scale, total_ref, own_hbm, uw_hbm, new_ref, search_ref, own_ref, uw_ref, sems):
    v = VECS
    copies = [
        pltpu.make_async_copy(own_hbm, own_ref, sems.at[0]),
        pltpu.make_async_copy(uw_hbm, uw_ref, sems.at[1]),
    ]
    for copy in copies:
        copy.start()
    coeffs, quotient = ritz_core(total_ref[...])
    coeffs = coeffs * scale
    quotient = jnp.broadcast_to(quotient, (v, 128))
    for copy in copies:
        copy.wait()
    for t in range(0, 32, 2):
        basis = []
        for i in (t, t + 1):
            search = uw_ref[i, :v] - quotient * uw_ref[i, v:]
            search_ref[pl.ds(i, v, stride=32), :] = search
            basis.append(jnp.concatenate([own_ref[i, :v], search, own_ref[i, v:]], axis=0))
        new = dots(coeffs, jnp.concatenate(basis, axis=1), ((1,), (0,)))
        new_ref[pl.ds(t, v, stride=32), :] = new[:, :128]
        new_ref[pl.ds(t + 1, v, stride=32), :] = new[:, 128:]


def finish_call(scale, total, own, uw):
    v = VECS
    vmem = pl.BlockSpec(memory_space=VMEM)
    hbm = pl.BlockSpec(memory_space=pl.ANY)
    out = jax.ShapeDtypeStruct((v * 32, 128), jnp.float32)
    return pl.pallas_call(
        lambda *refs: finish_kernel(scale, *refs),
        out_shape=(out, out),
        in_specs=[vmem, hbm, hbm],
        out_specs=(vmem, vmem),
        scratch_shapes=[
            VMEM((32, 2 * v, 128), jnp.float32),
            VMEM((32, 2 * v, 128), jnp.float32),
            pltpu.SemaphoreType.DMA((2,)),
        ],
        compiler_params=pltpu.CompilerParams(vmem_limit_bytes=12 * 2**20),
    )(total, own, uw)


def spread_sum(rows):
    plane = ("px", "pc")
    count = lax.axis_size("px") * lax.axis_size("pc")
    depth = lax.axis_size("pz")
    pieces = rows.reshape(count, -1, rows.shape[1])
    part = jnp.sum(lax.all_to_all(pieces, plane, 0, 0), axis=0)
    part = jnp.sum(
        lax.all_to_all(jnp.broadcast_to(part[None], (depth,) + part.shape), "pz", 0, 0), axis=0
    )
    whole = lax.all_to_all(jnp.broadcast_to(part[None], (count,) + part.shape), plane, 0, 0)
    return whole.reshape(rows.shape)


def neighbour(payload, step_a, step_b):
    count_a = lax.axis_size("px")
    count_b = lax.axis_size("pz") * lax.axis_size("pc")
    pairs = []
    for a in range(count_a):
        for b in range(count_b):
            if 0 <= a + step_a < count_a and 0 <= b + step_b < count_b:
                pairs.append(((a + step_a) * count_b + b + step_b, a * count_b + b))
    return lax.ppermute(payload, ("px", "pz", "pc"), pairs)


def shards(offsets, block, prior):
    v = block.shape[0]
    rows_a, rows_b, depth = block.shape[1:]
    total_a = rows_a * lax.axis_size("px")
    total_b = rows_b * lax.axis_size("pz") * lax.axis_size("pc")
    start = jnp.stack(
        [
            lax.axis_index("px") * rows_a,
            lax.axis_index(("pz", "pc")) * rows_b,
            jnp.int32(total_a),
            jnp.int32(total_b),
        ]
    ).astype(jnp.int32)
    own, down_a, up_a, down_b, up_b, c_pp, c_mm, c_pm, c_mp = pack_call(block, prior, offsets)
    pieces = (
        neighbour(down_a, 1, 0),
        neighbour(up_a, -1, 0),
        neighbour(down_b, 0, 1),
        neighbour(up_b, 0, -1),
        neighbour(c_pp, 1, 1),
        neighbour(c_mm, -1, -1),
        neighbour(c_pm, 1, -1),
        neighbour(c_mp, -1, 1),
    )
    gram, uw = gram_call(start, own, pieces, offsets)
    own = own.reshape(rows_a * rows_b, 2 * v, depth)
    scale = math.sqrt(total_a * total_b * depth)
    new_block, search = finish_call(scale, spread_sum(gram), own, uw)
    return (new_block.reshape(block.shape), search.reshape(block.shape))


def solution(mesh):
    grid = Mesh(
        mesh.devices.reshape(mesh.shape["px"], mesh.shape["py"] // 2, 2), ("px", "pz", "pc")
    )
    spec = P(None, "px", ("pz", "pc"), None)
    return jax.shard_map(
        shards, mesh=grid, in_specs=(spec, spec, spec), out_specs=(spec, spec), check_vma=False
    )
```

```python
import math

import jax
import jax.numpy as jnp
from jax import lax
from jax.experimental import pallas as pl
from jax.experimental.pallas import tpu as pltpu
from jax.sharding import Mesh
from jax.sharding import PartitionSpec as P

VECS = 48
HI = lax.Precision.HIGHEST
FORWARD = [(0, 0, 1), (0, 1, 0), (0, 1, 1), (1, 0, 0), (1, 0, 1), (1, 1, 0), (1, 1, 1)]
VMEM = pltpu.VMEM


def dots(a, b, dims):
    return lax.dot_general(a, b, (dims, ((), ())), precision=HI, preferred_element_type=jnp.float32)


def split(x):
    high = x.astype(jnp.bfloat16)
    return high, (x - high.astype(jnp.float32)).astype(jnp.bfloat16)


def split_dots(a, b, dims):
    (a_high, a_low), (b_high, b_low) = split(a), split(b)
    one = lambda x, y: lax.dot_general(
        x, y, (dims, ((), ())), preferred_element_type=jnp.float32
    )
    return one(a_high, b_high) + (one(a_high, b_low) + one(a_low, b_high))


def eliminated(gram):
    order = gram.shape[0]
    third = order // 3
    rows = lax.broadcasted_iota(jnp.int32, gram.shape, 0)
    cols = lax.broadcasted_iota(jnp.int32, gram.shape, 1)
    inverse = jnp.where(rows == cols, 1.0, 0.0).astype(jnp.float32)
    place = lax.broadcasted_iota(jnp.int32, (third, 128), 0)
    done = []
    for j in range(3):
        left = gram[:third]
        right = inverse[:third]
        gram = gram[third:]
        inverse = inverse[third:]
        pivots = jnp.ones((third, 128), jnp.float32)
        for k in range(0, third, 2):
            c = third * j + k
            first = jnp.broadcast_to(left[:, c : c + 1], (third, 128))
            second = jnp.broadcast_to(left[:, c + 1 : c + 2], (third, 128))
            p = first[k : k + 1, :]
            r = second[k : k + 1, :]
            s = second[k + 1 : k + 2, :]
            det = p * s - r * r
            inv = 1.0 / det
            ratio = r / p
            sp = s * inv
            rp = r * inv
            pp = p * inv
            one = jnp.where(place > k + 1, first * sp - second * rp, 0.0)
            one = jnp.where(place == k + 1, ratio, one)
            two = jnp.where(place > k + 1, second * pp - first * rp, 0.0)
            pivots = jnp.where(place == k, p, jnp.where(place == k + 1, s - r * ratio, pivots))
            one = jnp.concatenate([one, one], axis=1)
            two = jnp.concatenate([two, two], axis=1)
            left, right = (
                left - one * left[k : k + 1, :] - two * left[k + 1 : k + 2, :],
                right - one * right[k : k + 1, :] - two * right[k + 1 : k + 2, :],
            )
        scale = 1.0 / jnp.sqrt(pivots)
        scale = jnp.concatenate([scale, scale], axis=1)
        left = left * scale
        right = right * scale
        done.append(right)
        if j < 2:
            flipped = left.T[third * (j + 1) : order]
            gram = gram - dots(flipped, left, ((1,), (0,)))
            inverse = inverse - dots(flipped, right, ((1,), (0,)))
    return jnp.concatenate(done, axis=0)


def ritz_core(total):
    vecs = VECS
    order = 3 * vecs
    full = 4 * vecs
    rows = lax.broadcasted_iota(jnp.int32, total.shape, 0)
    cols = lax.broadcasted_iota(jnp.int32, total.shape, 1)
    flipped = total.T
    diagonal = total[full : full + 1, :]
    gram_k = jnp.where(rows <= cols, total, flipped)
    gram_m = jnp.where(rows > cols, total, jnp.where(rows == cols, diagonal, flipped))
    eye = rows == cols
    top = lambda g: jnp.sum(jnp.where(eye, g, 0.0)[:vecs], axis=1, keepdims=True)
    quotient = top(gram_k) / top(gram_m)

    def joined(g):
        mid = g[vecs : 2 * vecs] - quotient * g[2 * vecs : 3 * vecs]
        return jnp.concatenate([g[:vecs], mid, g[3 * vecs : full]], axis=0)

    gram_k = joined(joined(gram_k).T)
    gram_m = joined(joined(gram_m).T)
    gram_m = jnp.concatenate([gram_m, jnp.zeros((order, 256 - order), jnp.float32)], axis=1)
    inverse = eliminated(gram_m)[:, :order]
    half = dots(inverse, gram_k, ((1,), (0,)))
    reduced = dots(half, inverse, ((1,), (1,)))
    bound = jnp.max(jnp.sum(jnp.abs(reduced), axis=1, keepdims=True), axis=0, keepdims=True)
    eye = lax.broadcasted_iota(jnp.int32, (order, order), 0) == lax.broadcasted_iota(
        jnp.int32, (order, order), 1
    )
    shifted = jnp.where(eye, 1.0, 0.0) - reduced / bound
    filtered = dots(shifted[:vecs], shifted, ((1,), (0,)))
    return dots(filtered, inverse, ((1,), (0,))), quotient


def kuhn_tetrahedra():
    orders = [(0, 1, 2), (0, 2, 1), (1, 0, 2), (1, 2, 0), (2, 0, 1), (2, 1, 0)]
    tetrahedra = []
    for ordering in orders:
        corner = [0, 0, 0]
        corners = [(0, 0, 0)]
        for axis_step in ordering:
            corner[axis_step] = 1
            corners.append((corner[0], corner[1], corner[2]))
        tetrahedra.append(corners)
    return tetrahedra


def cross(p, q):
    return (
        p[1] * q[2] - p[2] * q[1],
        p[2] * q[0] - p[0] * q[2],
        p[0] * q[1] - p[1] * q[0],
    )


def dot3(p, q):
    return p[0] * q[0] + p[1] * q[1] + p[2] * q[2]


def shifted_lanes(x, step):
    return pltpu.roll(x, (-step) % x.shape[-1], x.ndim - 1)


def shifted_rows(x, step):
    return pltpu.roll(x, (-step) % x.shape[-2], x.ndim - 2)


def assemble_tables(off_ref, coef_ref, start_a, start_b, total_a, total_b):
    shape = (16, 128)
    row = lax.broadcasted_iota(jnp.int32, shape, 0)
    lane = lax.broadcasted_iota(jnp.int32, shape, 1)
    grid_b = start_b - 2 + row
    valid_bc = (grid_b >= 0) & (grid_b <= total_b - 2) & (row < 11) & (lane < 127)
    coef_ref[...] = jnp.zeros(coef_ref.shape, jnp.float32)

    def plane(a):
        grid_a = (start_a - 2 + a).astype(jnp.float32)
        base = [
            off_ref[0, a] + grid_a,
            off_ref[1, a] + grid_b.astype(jnp.float32),
            off_ref[2, a] + lane.astype(jnp.float32),
        ]
        out = {}
        for db in (0, 1):
            moved = [shifted_rows(p, db) if db else p for p in base]
            for dc in (0, 1):
                out[(db, dc)] = [shifted_lanes(p, dc) if dc else p for p in moved]
        return out

    def add(slot, a, value, b_shift, c_shift):
        if c_shift:
            value = shifted_lanes(value, -1)
        if b_shift == 0:
            value = shifted_rows(value, 1)
        coef_ref[slot, a] = coef_ref[slot, a] + value

    low = plane(0)
    for a in range(7):
        high = plane(a + 1)
        at = lambda corner: (high if corner[0] else low)[(corner[1], corner[2])]
        cell_a = start_a - 2 + a
        inside = valid_bc & (cell_a >= 0) & (cell_a <= total_a - 2)
        sums = {}
        for corners in kuhn_tetrahedra():
            anchor = at(corners[0])
            edges = [tuple(x - y for x, y in zip(at(c), anchor)) for c in corners[1:]]
            g1 = cross(edges[1], edges[2])
            g2 = cross(edges[2], edges[0])
            g3 = cross(edges[0], edges[1])
            g0 = tuple(-(x + y + z) for x, y, z in zip(g1, g2, g3))
            grads = [g0, g1, g2, g3]
            det = jnp.where(inside, jnp.abs(dot3(edges[0], g1)), 1.0)
            weight = jnp.where(inside, 1.0 / (6.0 * det), 0.0)
            for i in range(4):
                for j in range(i, 4):
                    step = tuple(q - p for p, q in zip(corners[i], corners[j]))
                    slot = 7 if i == j else FORWARD.index(step)
                    key = (slot, corners[i])
                    value = dot3(grads[i], grads[j]) * weight
                    sums[key] = sums[key] + value if key in sums else value
            part = jnp.where(inside, det * (1.0 / 24.0), 0.0)
            for corner in corners:
                key = (8, corner)
                sums[key] = sums[key] + part if key in sums else part
        for (slot, corner), value in sums.items():
            table_a = a + corner[0] - 1
            if 0 <= table_a <= 5:
                add(slot, table_a, value, corner[1], corner[2])
        low = high


def pack_kernel(block_ref, prior_ref, off_ref, down_a, up_a, down_b, up_b, c_pp, c_mm, c_pm, c_mp):
    v = VECS
    block = lambda a, b: block_ref[pl.ds(a * 8 + b, v, stride=32), :]
    prior = lambda a, b: prior_ref[pl.ds(a * 8 + b, v, stride=32), :]
    for a in range(4):
        for b in range(8):
            if a in (2,) and b not in (0, 1, 7):
                continue
            x = block(a, b)
            if a == 0 or b == 0:
                y = prior(a, b)
            if a < 2:
                down_a[a * 8 + b] = x
            if a == 0:
                down_a[16 + b] = y
            if a == 3:
                up_a[b] = x
            if b < 2:
                down_b[b * 4 + a] = x
            if b == 0:
                down_b[8 + a] = y
            if b == 7:
                up_b[a] = x
            if a < 2 and b < 2:
                c_pp[a * 2 + b] = x
            if a == 0 and b == 0:
                c_pp[4] = y
            if a == 3 and b == 7:
                c_mm[0] = x
            if a == 0 and b == 7:
                c_pm[0] = x
            if a == 3 and b == 0:
                c_mp[0] = x
    for i in range(3):
        for a in range(4):
            down_b[12, i * 8 + a * 2 : i * 8 + a * 2 + 2] = off_ref[i, a, 0:2]
            up_b[4, i * 8 + a * 2 : i * 8 + a * 2 + 2] = off_ref[i, a, 6:8]
        for a in range(2):
            down_a[24, i * 16 + a * 8 : i * 16 + a * 8 + 8] = off_ref[i, a]
            up_a[8, i * 16 + a * 8 : i * 16 + a * 8 + 8] = off_ref[i, 2 + a]
            pair = slice(i * 4 + a * 2, i * 4 + a * 2 + 2)
            c_pp[5, pair] = off_ref[i, a, 0:2]
            c_mm[1, pair] = off_ref[i, 2 + a, 6:8]
            c_pm[1, pair] = off_ref[i, a, 6:8]
            c_mp[1, pair] = off_ref[i, 2 + a, 0:2]


def pack_call(block, prior, offsets):
    v = VECS
    vmem = pl.BlockSpec(memory_space=VMEM)
    sizes = [(n, v, 128) for n in (25, 9, 13, 5, 6, 2, 2, 2)]
    return pl.pallas_call(
        pack_kernel,
        out_shape=tuple(jax.ShapeDtypeStruct(s, jnp.float32) for s in sizes),
        in_specs=[vmem] * 3,
        out_specs=(vmem,) * len(sizes),
        compiler_params=pltpu.CompilerParams(vmem_limit_bytes=60 * 2**20),
    )(block.reshape(-1, 128), prior.reshape(-1, 128), offsets)


def gram_kernel(start_ref, block_hbm, prior_hbm, down_a, up_a, down_b, up_b, c_pp, c_mm, c_pm, c_mp, off_own,
                gram_ref, basis_hbm, block_ref, prior_ref, edge_ref, off_ref, coef_ref, turn_ref, xb_ref, y_ref, acc_ref,
                sems):
    v = VECS
    moves = [
        (piece.at[piece.shape[0] - 1], edge_ref.at[i])
        for i, piece in enumerate((down_a, up_a, down_b, up_b, c_pp, c_mm, c_pm, c_mp))
    ]
    third = slice(2 * v, 3 * v)
    moves += [(block_hbm, block_ref), (prior_hbm, prior_ref)]
    moves += [
        (down_a.at[0:8], xb_ref.at[5, 1:9]),
        (down_a.at[8:16], xb_ref.at[6, 1:9]),
        (up_a.at[0:8], xb_ref.at[0, 1:9]),
        (down_b.at[0:4], xb_ref.at[1:5, 9]),
        (down_b.at[4:8], xb_ref.at[1:5, 10]),
        (up_b.at[0:4], xb_ref.at[1:5, 0]),
        (c_pp.at[0:2], xb_ref.at[5, 9:11]),
        (c_pp.at[2:4], xb_ref.at[6, 9:11]),
        (c_mm.at[0], xb_ref.at[0, 0]),
        (c_pm.at[0], xb_ref.at[5, 0]),
        (c_mp.at[0], xb_ref.at[0, 9]),
        (down_a.at[16:24], y_ref.at[4, 0:8, third]),
        (down_b.at[8:12], y_ref.at[0:4, 8, third]),
        (c_pp.at[4], y_ref.at[4, 8, third]),
    ]
    copies = [pltpu.make_async_copy(x, y, sems.at[i]) for i, (x, y) in enumerate(moves)]
    for copy in copies:
        copy.start()
    for copy in copies[8:10]:
        copy.wait()
    for a in range(4):
        for b in range(8):
            rows = pl.ds(a * 8 + b, v, stride=32)
            xb_ref[a + 1, b + 1] = block_ref[rows, :]
            y_ref[a, b, third] = prior_ref[rows, :]
    for copy in copies[:8]:
        copy.wait()
    for i in range(3):
        for a in range(4):
            off_ref[i, 2 + a, 2:10] = off_own[i, a]
            pair = slice(i * 8 + a * 2, i * 8 + a * 2 + 2)
            off_ref[i, 2 + a, 10:12] = edge_ref[2, pair]
            off_ref[i, 2 + a, 0:2] = edge_ref[3, pair]
        for a in range(2):
            rows = slice(i * 16 + a * 8, i * 16 + a * 8 + 8)
            off_ref[i, 6 + a, 2:10] = edge_ref[0, rows]
            off_ref[i, a, 2:10] = edge_ref[1, rows]
            pair = slice(i * 4 + a * 2, i * 4 + a * 2 + 2)
            off_ref[i, 6 + a, 10:12] = edge_ref[4, pair]
            off_ref[i, a, 0:2] = edge_ref[5, pair]
            off_ref[i, 6 + a, 0:2] = edge_ref[6, pair]
            off_ref[i, a, 10:12] = edge_ref[7, pair]
    assemble_tables(off_ref, coef_ref, start_ref[0], start_ref[1], start_ref[2], start_ref[3])
    for slot, (da, db, dc) in enumerate(FORWARD):
        if dc:
            for a in range(6):
                turn_ref[slot, a] = shifted_lanes(coef_ref[slot, a], -1)
    for copy in copies[10:]:
        copy.wait()

    def row(ref, slot, a, b):
        return ref[slot, a, pl.ds(b, 1), :]

    def k_block(a, b):
        x = lambda i, j: xb_ref[a + 1 + i, b + 1 + j]
        total = x(0, 0) * row(coef_ref, 7, a + 1, b + 1)
        ahead = None
        behind = None
        for slot, (da, db, dc) in enumerate(FORWARD):
            front = x(da, db) * row(turn_ref if dc else coef_ref, slot, a + 1, b + 1)
            back = x(-da, -db) * row(coef_ref, slot, a + 1 - da, b + 1 - db)
            if dc:
                ahead = front if ahead is None else ahead + front
                behind = back if behind is None else behind + back
            else:
                total = total + front + back
        return total + shifted_lanes(ahead, 1) + shifted_lanes(behind, -1)

    def first(t, carry):
        a = t // 9
        b = t - a * 9
        kb = k_block(a, b)
        diagonal = row(coef_ref, 7, a + 1, b + 1)
        inverse = 1.0 / jnp.where(diagonal == 0.0, 1.0, diagonal)
        y_ref[a, b, :v] = kb * inverse
        y_ref[a, b, v : 2 * v] = xb_ref[a + 1, b + 1] * (row(coef_ref, 8, a + 1, b + 1) * inverse)
        return carry

    lax.fori_loop(0, 45, first, 0, unroll=3)
    results = [
        pltpu.make_async_copy(x, basis_hbm.at[:, :, rows], sems.at[24 + i])
        for i, (x, rows) in enumerate(
            ((xb_ref.at[1:5, 1:9], slice(0, v)), (y_ref.at[0:4, 0:8], slice(v, 4 * v)))
        )
    ]
    for copy in results:
        copy.start()

    acc_ref[...] = jnp.zeros(acc_ref.shape, jnp.float32)

    def sides(a, b):
        block = xb_ref[a + 1, b + 1]
        y = y_ref[a, b]
        diagonal = row(coef_ref, 7, a + 1, b + 1)
        mass = row(coef_ref, 8, a + 1, b + 1)
        straight = y * (0.5 * diagonal)
        ahead = None
        for slot, (da, db, dc) in enumerate(FORWARD):
            front = y_ref[a + da, b + db] * row(turn_ref if dc else coef_ref, slot, a + 1, b + 1)
            if dc:
                ahead = front if ahead is None else ahead + front
            else:
                straight = straight + front
        ky = straight + shifted_lanes(ahead, 1)
        kb = y[:v] * diagonal
        basis = jnp.concatenate([block, y], axis=0)
        return basis, jnp.concatenate([kb, ky, basis * mass], axis=0)

    def second(t, carry):
        a = t // 4
        b = (t - a * 4) * 2
        x0, r0 = sides(a, b)
        x1, r1 = sides(a, b + 1)
        left = jnp.concatenate([r0, r1], axis=1)
        right = jnp.concatenate([x0, x1], axis=1)
        acc_ref[...] += split_dots(left, right, ((1,), (1,)))
        return carry

    lax.fori_loop(0, 16, second, 0)

    n = 4 * v
    acc = acc_ref[...]
    pad = lambda g: jnp.concatenate(
        [jnp.concatenate([g, jnp.zeros((n, 256 - n), jnp.float32)], axis=1),
         jnp.zeros((256 - n, 256), jnp.float32)], axis=0)
    half = pad(acc[:n])
    gram_m = pad(acc[n:])
    rows = lax.broadcasted_iota(jnp.int32, (256, 256), 0)
    cols = lax.broadcasted_iota(jnp.int32, (256, 256), 1)
    gram_k = jnp.where(rows < v, half, half + half.T)
    diagonal = jnp.sum(jnp.where(rows == cols, gram_m, 0.0), axis=0, keepdims=True)
    square = jnp.where(rows <= cols, gram_k, gram_m)
    gram_ref[...] = jnp.where(rows < n, square, diagonal)
    for copy in results:
        copy.wait()


def gram_call(start, block, prior, pieces, off):
    v = VECS
    spec = pl.BlockSpec(memory_space=VMEM)
    return pl.pallas_call(
        gram_kernel,
        out_shape=(
            jax.ShapeDtypeStruct((256, 256), jnp.float32),
            jax.ShapeDtypeStruct((4, 8, 4 * v, 128), jnp.float32),
        ),
        in_specs=[pl.BlockSpec(memory_space=pltpu.SMEM)]
        + [pl.BlockSpec(memory_space=pl.ANY)] * (2 + len(pieces))
        + [spec],
        out_specs=(spec, pl.BlockSpec(memory_space=pl.ANY)),
        scratch_shapes=[
            VMEM((32 * v, 128), jnp.float32),
            VMEM((32 * v, 128), jnp.float32),
            VMEM((8, v, 128), jnp.float32),
            VMEM((3, 8, 16, 128), jnp.float32),
            VMEM((9, 6, 16, 128), jnp.float32),
            VMEM((7, 6, 16, 128), jnp.float32),
            VMEM((7, 11, v, 128), jnp.float32),
            VMEM((5, 9, 3 * v, 128), jnp.float32),
            VMEM((8 * v, 4 * v), jnp.float32),
            pltpu.SemaphoreType.DMA((26,)),
        ],
        compiler_params=pltpu.CompilerParams(vmem_limit_bytes=52 * 2**20),
    )(start, block.reshape(-1, 128), prior.reshape(-1, 128), *pieces, off)


def finish_kernel(scale, total_ref, basis_hbm, new_ref, search_ref, basis_ref, sem):
    v = VECS
    load = pltpu.make_async_copy(basis_hbm, basis_ref, sem)
    load.start()
    coeffs, quotient = ritz_core(total_ref[...])
    coeffs = coeffs * scale
    quotient = jnp.broadcast_to(quotient, (v, 128))
    load.wait()
    for t in range(0, 32, 2):
        basis = []
        for i in (t, t + 1):
            x = basis_ref[i // 8, i % 8]
            search = x[v : 2 * v] - quotient * x[2 * v : 3 * v]
            search_ref[pl.ds(i, v, stride=32), :] = search
            basis.append(jnp.concatenate([x[:v], search, x[3 * v :]], axis=0))
        new = split_dots(coeffs, jnp.concatenate(basis, axis=1), ((1,), (0,)))
        new_ref[pl.ds(t, v, stride=32), :] = new[:, :128]
        new_ref[pl.ds(t + 1, v, stride=32), :] = new[:, 128:]


def finish_call(scale, total, basis):
    v = VECS
    vmem = pl.BlockSpec(memory_space=VMEM)
    out = jax.ShapeDtypeStruct((v * 32, 128), jnp.float32)
    return pl.pallas_call(
        lambda *refs: finish_kernel(scale, *refs),
        out_shape=(out, out),
        in_specs=[vmem, pl.BlockSpec(memory_space=pl.ANY)],
        out_specs=(vmem, vmem),
        scratch_shapes=[VMEM((4, 8, 4 * v, 128), jnp.float32), pltpu.SemaphoreType.DMA],
        compiler_params=pltpu.CompilerParams(vmem_limit_bytes=60 * 2**20),
    )(total, basis)


def spread_sum(rows):
    plane = ("px", "pc")
    count = lax.axis_size("px") * lax.axis_size("pc")
    depth = lax.axis_size("pz")
    pieces = rows.reshape(count, -1, rows.shape[1])
    part = jnp.sum(lax.all_to_all(pieces, plane, 0, 0), axis=0)
    part = jnp.sum(
        lax.all_to_all(jnp.broadcast_to(part[None], (depth,) + part.shape), "pz", 0, 0), axis=0
    )
    whole = lax.all_to_all(jnp.broadcast_to(part[None], (count,) + part.shape), plane, 0, 0)
    return whole.reshape(rows.shape)


def neighbour(payload, step_a, step_b):
    count_a = lax.axis_size("px")
    count_b = lax.axis_size("pz") * lax.axis_size("pc")
    pairs = []
    for a in range(count_a):
        for b in range(count_b):
            if 0 <= a + step_a < count_a and 0 <= b + step_b < count_b:
                pairs.append(((a + step_a) * count_b + b + step_b, a * count_b + b))
    return lax.ppermute(payload, ("px", "pz", "pc"), pairs)


def shards(offsets, block, prior):
    rows_a, rows_b, depth = block.shape[1:]
    total_a = rows_a * lax.axis_size("px")
    total_b = rows_b * lax.axis_size("pz") * lax.axis_size("pc")
    start = jnp.stack(
        [
            lax.axis_index("px") * rows_a,
            lax.axis_index(("pz", "pc")) * rows_b,
            jnp.int32(total_a),
            jnp.int32(total_b),
        ]
    ).astype(jnp.int32)
    down_a, up_a, down_b, up_b, c_pp, c_mm, c_pm, c_mp = pack_call(block, prior, offsets)
    pieces = (
        neighbour(down_a, 1, 0),
        neighbour(up_a, -1, 0),
        neighbour(down_b, 0, 1),
        neighbour(up_b, 0, -1),
        neighbour(c_pp, 1, 1),
        neighbour(c_mm, -1, -1),
        neighbour(c_pm, 1, -1),
        neighbour(c_mp, -1, 1),
    )
    gram, basis = gram_call(start, block, prior, pieces, offsets)
    scale = math.sqrt(total_a * total_b * depth)
    new_block, search = finish_call(scale, spread_sum(gram), basis)
    return (new_block.reshape(block.shape), search.reshape(block.shape))


def solution(mesh):
    grid = Mesh(
        mesh.devices.reshape(mesh.shape["px"], mesh.shape["py"] // 2, 2), ("px", "pz", "pc")
    )
    spec = P(None, "px", ("pz", "pc"), None)
    return jax.shard_map(
        shards, mesh=grid, in_specs=(spec, spec, spec), out_specs=(spec, spec), check_vma=False
    )
```

```python
import math

import jax
import jax.numpy as jnp
from jax import lax
from jax.experimental import pallas as pl
from jax.experimental.pallas import tpu as pltpu
from jax.sharding import Mesh
from jax.sharding import PartitionSpec as P

VECS = 48
HI = lax.Precision.HIGHEST
FORWARD = [(0, 0, 1), (0, 1, 0), (0, 1, 1), (1, 0, 0), (1, 0, 1), (1, 1, 0), (1, 1, 1)]
VMEM = pltpu.VMEM


def dots(a, b, dims):
    return lax.dot_general(a, b, (dims, ((), ())), precision=HI, preferred_element_type=jnp.float32)


def split(x):
    high = x.astype(jnp.bfloat16)
    return high, (x - high.astype(jnp.float32)).astype(jnp.bfloat16)


def split_dots(a, b, dims):
    (a_high, a_low), (b_high, b_low) = split(a), split(b)
    one = lambda x, y: lax.dot_general(
        x, y, (dims, ((), ())), preferred_element_type=jnp.float32
    )
    return one(a_high, b_high) + (one(a_high, b_low) + one(a_low, b_high))


def pair_factors(first, second, k, place, pivots):
    p = first[k : k + 1, :]
    r = second[k : k + 1, :]
    s = second[k + 1 : k + 2, :]
    inv = 1.0 / (p * s - r * r)
    ratio = r / p
    one = jnp.where(place > k + 1, first * (s * inv) - second * (r * inv), 0.0)
    one = jnp.where(place == k + 1, ratio, one)
    two = jnp.where(place > k + 1, second * (p * inv) - first * (r * inv), 0.0)
    pivots = jnp.where(place == k, p, jnp.where(place == k + 1, s - r * ratio, pivots))
    return one, two, pivots


def eliminated(gram):
    order = gram.shape[0]
    third = order // 3
    rows = lax.broadcasted_iota(jnp.int32, gram.shape, 0)
    cols = lax.broadcasted_iota(jnp.int32, gram.shape, 1)
    inverse = jnp.where(rows == cols, 1.0, 0.0).astype(jnp.float32)
    place = lax.broadcasted_iota(jnp.int32, (third, 128), 0)
    done = []
    for j in range(3):
        left = gram[:third]
        right = inverse[:third]
        gram = gram[third:]
        inverse = inverse[third:]
        pivots = jnp.ones((third, 128), jnp.float32)
        for k in range(0, third, 4):
            c = third * j + k
            columns = [
                jnp.broadcast_to(left[:, c + i : c + i + 1], (third, 128)) for i in range(4)
            ]
            one, two, pivots = pair_factors(columns[0], columns[1], k, place, pivots)
            columns = [
                x - one * x[k : k + 1, :] - two * x[k + 1 : k + 2, :] for x in columns[2:]
            ]
            three, four, pivots = pair_factors(columns[0], columns[1], k + 2, place, pivots)
            one, two, three, four = [
                jnp.concatenate([x, x], axis=1) for x in (one, two, three, four)
            ]
            left = left - one * left[k : k + 1, :] - two * left[k + 1 : k + 2, :]
            right = right - one * right[k : k + 1, :] - two * right[k + 1 : k + 2, :]
            left = left - three * left[k + 2 : k + 3, :] - four * left[k + 3 : k + 4, :]
            right = right - three * right[k + 2 : k + 3, :] - four * right[k + 3 : k + 4, :]
        scale = 1.0 / jnp.sqrt(pivots)
        scale = jnp.concatenate([scale, scale], axis=1)
        left = left * scale
        right = right * scale
        done.append(right)
        if j < 2:
            flipped = left.T[third * (j + 1) : order]
            gram = gram - dots(flipped, left, ((1,), (0,)))
            inverse = inverse - dots(flipped, right, ((1,), (0,)))
    return jnp.concatenate(done, axis=0)


def ritz_core(total):
    vecs = VECS
    order = 3 * vecs
    full = 4 * vecs
    rows = lax.broadcasted_iota(jnp.int32, total.shape, 0)
    cols = lax.broadcasted_iota(jnp.int32, total.shape, 1)
    flipped = total.T
    diagonal = total[full : full + 1, :]
    gram_k = jnp.where(rows <= cols, total, flipped)
    gram_m = jnp.where(rows > cols, total, jnp.where(rows == cols, diagonal, flipped))
    eye = rows == cols
    top = lambda g: jnp.sum(jnp.where(eye, g, 0.0)[:vecs], axis=1, keepdims=True)
    quotient = top(gram_k) / top(gram_m)

    def joined(g):
        mid = g[vecs : 2 * vecs] - quotient * g[2 * vecs : 3 * vecs]
        return jnp.concatenate([g[:vecs], mid, g[3 * vecs : full]], axis=0)

    gram_k = joined(joined(gram_k).T)
    gram_m = joined(joined(gram_m).T)
    gram_m = jnp.concatenate([gram_m, jnp.zeros((order, 256 - order), jnp.float32)], axis=1)
    inverse = eliminated(gram_m)[:, :order]
    half = dots(inverse, gram_k, ((1,), (0,)))
    reduced = dots(half, inverse, ((1,), (1,)))
    bound = jnp.max(jnp.sum(jnp.abs(reduced), axis=1, keepdims=True), axis=0, keepdims=True)
    eye = lax.broadcasted_iota(jnp.int32, (order, order), 0) == lax.broadcasted_iota(
        jnp.int32, (order, order), 1
    )
    shifted = jnp.where(eye, 1.0, 0.0) - reduced / bound
    filtered = dots(shifted[:vecs], shifted, ((1,), (0,)))
    return dots(filtered, inverse, ((1,), (0,))), quotient


def kuhn_tetrahedra():
    orders = [(0, 1, 2), (0, 2, 1), (1, 0, 2), (1, 2, 0), (2, 0, 1), (2, 1, 0)]
    tetrahedra = []
    for ordering in orders:
        corner = [0, 0, 0]
        corners = [(0, 0, 0)]
        for axis_step in ordering:
            corner[axis_step] = 1
            corners.append((corner[0], corner[1], corner[2]))
        tetrahedra.append(corners)
    return tetrahedra


def cross(p, q):
    return (
        p[1] * q[2] - p[2] * q[1],
        p[2] * q[0] - p[0] * q[2],
        p[0] * q[1] - p[1] * q[0],
    )


def dot3(p, q):
    return p[0] * q[0] + p[1] * q[1] + p[2] * q[2]


def shifted_lanes(x, step):
    return pltpu.roll(x, (-step) % x.shape[-1], x.ndim - 1)


def shifted_rows(x, step):
    return pltpu.roll(x, (-step) % x.shape[-2], x.ndim - 2)


def assemble_tables(off_ref, coef_ref, start_a, start_b, total_a, total_b):
    shape = (16, 128)
    row = lax.broadcasted_iota(jnp.int32, shape, 0)
    lane = lax.broadcasted_iota(jnp.int32, shape, 1)
    grid_b = start_b - 2 + row
    valid_bc = (grid_b >= 0) & (grid_b <= total_b - 2) & (row < 11) & (lane < 127)
    coef_ref[...] = jnp.zeros(coef_ref.shape, jnp.float32)

    def plane(a):
        grid_a = (start_a - 2 + a).astype(jnp.float32)
        base = [
            off_ref[0, a] + grid_a,
            off_ref[1, a] + grid_b.astype(jnp.float32),
            off_ref[2, a] + lane.astype(jnp.float32),
        ]
        out = {}
        for db in (0, 1):
            moved = [shifted_rows(p, db) if db else p for p in base]
            for dc in (0, 1):
                out[(db, dc)] = [shifted_lanes(p, dc) if dc else p for p in moved]
        return out

    def add(slot, a, value, b_shift, c_shift):
        if c_shift:
            value = shifted_lanes(value, -1)
        if b_shift == 0:
            value = shifted_rows(value, 1)
        coef_ref[slot, a] = coef_ref[slot, a] + value

    low = plane(0)
    for a in range(7):
        high = plane(a + 1)
        at = lambda corner: (high if corner[0] else low)[(corner[1], corner[2])]
        cell_a = start_a - 2 + a
        inside = valid_bc & (cell_a >= 0) & (cell_a <= total_a - 2)
        sums = {}
        for corners in kuhn_tetrahedra():
            anchor = at(corners[0])
            edges = [tuple(x - y for x, y in zip(at(c), anchor)) for c in corners[1:]]
            g1 = cross(edges[1], edges[2])
            g2 = cross(edges[2], edges[0])
            g3 = cross(edges[0], edges[1])
            g0 = tuple(-(x + y + z) for x, y, z in zip(g1, g2, g3))
            grads = [g0, g1, g2, g3]
            det = jnp.where(inside, jnp.abs(dot3(edges[0], g1)), 1.0)
            weight = jnp.where(inside, 1.0 / (6.0 * det), 0.0)
            for i in range(4):
                for j in range(i, 4):
                    step = tuple(q - p for p, q in zip(corners[i], corners[j]))
                    slot = 7 if i == j else FORWARD.index(step)
                    key = (slot, corners[i])
                    value = dot3(grads[i], grads[j]) * weight
                    sums[key] = sums[key] + value if key in sums else value
            part = jnp.where(inside, det * (1.0 / 24.0), 0.0)
            for corner in corners:
                key = (8, corner)
                sums[key] = sums[key] + part if key in sums else part
        for (slot, corner), value in sums.items():
            table_a = a + corner[0] - 1
            if 0 <= table_a <= 5:
                add(slot, table_a, value, corner[1], corner[2])
        low = high


DOWN_B = [(0, 0), (0, 1), (1, 0), (1, 1)]
REST_B = [(2, 0), (2, 1), (3, 1), (3, 0)]
UP_B = {0: 0, 3: 2, 1: 3, 2: 4}


def place_b(a, b):
    return DOWN_B.index((a, b)) if (a, b) in DOWN_B else 9 + REST_B.index((a, b))


def pack_kernel(block_ref, prior_ref, off_ref, down_a, up_a, down_b, up_b):
    v = VECS
    block = lambda a, b: block_ref[pl.ds(a * 8 + b, v, stride=32), :]
    prior = lambda a, b: prior_ref[pl.ds(a * 8 + b, v, stride=32), :]
    for a in range(4):
        for b in range(8):
            if a == 2 and b not in (0, 1, 7):
                continue
            x = block(a, b)
            if a == 0 or b == 0:
                y = prior(a, b)
            if a < 2:
                down_a[a * 8 + b] = x
            if a == 0:
                down_a[16 + b] = y
            if a == 3:
                up_a[b] = x
            if b < 2:
                down_b[place_b(a, b)] = x
            if b == 0:
                down_b[4 if a == 0 else 5 + a] = y
            if b == 7:
                up_b[UP_B[a]] = x
    for i in range(3):
        for a in range(4):
            down_b[5, i * 8 + a * 2 : i * 8 + a * 2 + 2] = off_ref[i, a, 0:2]
            up_b[1, i * 8 + a * 2 : i * 8 + a * 2 + 2] = off_ref[i, a, 6:8]
        for a in range(2):
            down_a[24, i * 16 + a * 8 : i * 16 + a * 8 + 8] = off_ref[i, a]
            up_a[8, i * 16 + a * 8 : i * 16 + a * 8 + 8] = off_ref[i, 2 + a]


def pack_call(block, prior, offsets):
    v = VECS
    vmem = pl.BlockSpec(memory_space=VMEM)
    sizes = [(n, v, 128) for n in (25, 9, 13, 5)]
    return pl.pallas_call(
        pack_kernel,
        out_shape=tuple(jax.ShapeDtypeStruct(s, jnp.float32) for s in sizes),
        in_specs=[vmem] * 3,
        out_specs=(vmem,) * len(sizes),
        compiler_params=pltpu.CompilerParams(vmem_limit_bytes=60 * 2**20),
    )(block.reshape(-1, 128), prior.reshape(-1, 128), offsets)


def gram_kernel(start_ref, block_hbm, prior_hbm, down_a, up_a, down_b, up_b, down_c, up_c, off_own,
                gram_ref, basis_hbm, block_ref, prior_ref, edge_ref, off_ref, coef_ref, turn_ref, xb_ref, y_ref, acc_ref,
                sems):
    v = VECS
    edges = (down_a.at[24], up_a.at[8], down_b.at[5], up_b.at[1],
             down_c.at[5], up_c.at[3], down_c.at[7], up_c.at[1])
    moves = [(piece, edge_ref.at[i]) for i, piece in enumerate(edges)]
    third = slice(2 * v, 3 * v)
    moves += [(block_hbm, block_ref), (prior_hbm, prior_ref)]
    moves += [
        (down_a.at[0:8], xb_ref.at[5, 1:9]),
        (down_a.at[8:16], xb_ref.at[6, 1:9]),
        (up_a.at[0:8], xb_ref.at[0, 1:9]),
        (down_b.at[0:2], xb_ref.at[1, 9:11]),
        (down_b.at[2:4], xb_ref.at[2, 9:11]),
        (down_b.at[9:11], xb_ref.at[3, 9:11]),
        (down_b.at[11], xb_ref.at[4, 10]),
        (down_b.at[12], xb_ref.at[4, 9]),
        (up_b.at[0], xb_ref.at[1, 0]),
        (up_b.at[3:5], xb_ref.at[2:4, 0]),
        (up_b.at[2], xb_ref.at[4, 0]),
        (down_c.at[0:2], xb_ref.at[5, 9:11]),
        (down_c.at[2:4], xb_ref.at[6, 9:11]),
        (up_c.at[2], xb_ref.at[0, 0]),
        (down_c.at[6], xb_ref.at[5, 0]),
        (up_c.at[0], xb_ref.at[0, 9]),
        (down_a.at[16:24], y_ref.at[4, 0:8, third]),
        (down_b.at[4], y_ref.at[0, 8, third]),
        (down_b.at[6:9], y_ref.at[1:4, 8, third]),
        (down_c.at[4], y_ref.at[4, 8, third]),
    ]
    copies = [pltpu.make_async_copy(x, y, sems.at[i]) for i, (x, y) in enumerate(moves)]
    for copy in copies:
        copy.start()
    for copy in copies[8:10]:
        copy.wait()
    for a in range(4):
        for b in range(8):
            rows = pl.ds(a * 8 + b, v, stride=32)
            xb_ref[a + 1, b + 1] = block_ref[rows, :]
            y_ref[a, b, third] = prior_ref[rows, :]
    for copy in copies[:8]:
        copy.wait()
    for i in range(3):
        for a in range(4):
            off_ref[i, 2 + a, 2:10] = off_own[i, a]
            pair = slice(i * 8 + a * 2, i * 8 + a * 2 + 2)
            off_ref[i, 2 + a, 10:12] = edge_ref[2, pair]
            off_ref[i, 2 + a, 0:2] = edge_ref[3, pair]
        for a in range(2):
            rows = slice(i * 16 + a * 8, i * 16 + a * 8 + 8)
            off_ref[i, 6 + a, 2:10] = edge_ref[0, rows]
            off_ref[i, a, 2:10] = edge_ref[1, rows]
            low = slice(i * 8 + a * 2, i * 8 + a * 2 + 2)
            high = slice(i * 8 + a * 2 + 4, i * 8 + a * 2 + 6)
            off_ref[i, 6 + a, 10:12] = edge_ref[4, low]
            off_ref[i, a, 0:2] = edge_ref[5, high]
            off_ref[i, 6 + a, 0:2] = edge_ref[6, low]
            off_ref[i, a, 10:12] = edge_ref[7, high]
    assemble_tables(off_ref, coef_ref, start_ref[0], start_ref[1], start_ref[2], start_ref[3])
    for slot, (da, db, dc) in enumerate(FORWARD):
        if dc:
            for a in range(6):
                turn_ref[slot, a] = shifted_lanes(coef_ref[slot, a], -1)
    for copy in copies[10:]:
        copy.wait()

    def row(ref, slot, a, b):
        return ref[slot, a, pl.ds(b, 1), :]

    def k_block(a, b):
        x = lambda i, j: xb_ref[a + 1 + i, b + 1 + j]
        total = x(0, 0) * row(coef_ref, 7, a + 1, b + 1)
        ahead = None
        behind = None
        for slot, (da, db, dc) in enumerate(FORWARD):
            front = x(da, db) * row(turn_ref if dc else coef_ref, slot, a + 1, b + 1)
            back = x(-da, -db) * row(coef_ref, slot, a + 1 - da, b + 1 - db)
            if dc:
                ahead = front if ahead is None else ahead + front
                behind = back if behind is None else behind + back
            else:
                total = total + front + back
        return total + shifted_lanes(ahead, 1) + shifted_lanes(behind, -1)

    def first(t, carry):
        a = t // 9
        b = t - a * 9
        kb = k_block(a, b)
        diagonal = row(coef_ref, 7, a + 1, b + 1)
        inverse = 1.0 / jnp.where(diagonal == 0.0, 1.0, diagonal)
        y_ref[a, b, :v] = kb * inverse
        y_ref[a, b, v : 2 * v] = xb_ref[a + 1, b + 1] * (row(coef_ref, 8, a + 1, b + 1) * inverse)
        return carry

    lax.fori_loop(0, 45, first, 0, unroll=9)
    results = [
        pltpu.make_async_copy(x, basis_hbm.at[:, :, rows], sems.at[30 + i])
        for i, (x, rows) in enumerate(
            ((xb_ref.at[1:5, 1:9], slice(0, v)), (y_ref.at[0:4, 0:8], slice(v, 4 * v)))
        )
    ]
    for copy in results:
        copy.start()

    acc_ref[...] = jnp.zeros(acc_ref.shape, jnp.float32)

    def sides(a, b):
        block = xb_ref[a + 1, b + 1]
        y = y_ref[a, b]
        diagonal = row(coef_ref, 7, a + 1, b + 1)
        mass = row(coef_ref, 8, a + 1, b + 1)
        straight = y * (0.5 * diagonal)
        ahead = None
        for slot, (da, db, dc) in enumerate(FORWARD):
            front = y_ref[a + da, b + db] * row(turn_ref if dc else coef_ref, slot, a + 1, b + 1)
            if dc:
                ahead = front if ahead is None else ahead + front
            else:
                straight = straight + front
        ky = straight + shifted_lanes(ahead, 1)
        kb = y[:v] * diagonal
        basis = jnp.concatenate([block, y], axis=0)
        return basis, jnp.concatenate([kb, ky, basis * mass], axis=0)

    def second(t, carry):
        a = t // 4
        b = (t - a * 4) * 2
        x0, r0 = sides(a, b)
        x1, r1 = sides(a, b + 1)
        left = jnp.concatenate([r0, r1], axis=1)
        right = jnp.concatenate([x0, x1], axis=1)
        acc_ref[...] += split_dots(left, right, ((1,), (1,)))
        return carry

    lax.fori_loop(0, 16, second, 0, unroll=4)

    n = 4 * v
    acc = acc_ref[...]
    pad = lambda g: jnp.concatenate(
        [jnp.concatenate([g, jnp.zeros((n, 256 - n), jnp.float32)], axis=1),
         jnp.zeros((256 - n, 256), jnp.float32)], axis=0)
    half = pad(acc[:n])
    gram_m = pad(acc[n:])
    rows = lax.broadcasted_iota(jnp.int32, (256, 256), 0)
    cols = lax.broadcasted_iota(jnp.int32, (256, 256), 1)
    gram_k = jnp.where(rows < v, half, half + half.T)
    diagonal = jnp.sum(jnp.where(rows == cols, gram_m, 0.0), axis=0, keepdims=True)
    square = jnp.where(rows <= cols, gram_k, gram_m)
    gram_ref[...] = jnp.where(rows < n, square, diagonal)
    for copy in results:
        copy.wait()


def gram_call(start, block, prior, pieces, off):
    v = VECS
    spec = pl.BlockSpec(memory_space=VMEM)
    return pl.pallas_call(
        gram_kernel,
        out_shape=(
            jax.ShapeDtypeStruct((256, 256), jnp.float32),
            jax.ShapeDtypeStruct((4, 8, 4 * v, 128), jnp.float32),
        ),
        in_specs=[pl.BlockSpec(memory_space=pltpu.SMEM)]
        + [pl.BlockSpec(memory_space=pl.ANY)] * (2 + len(pieces))
        + [spec],
        out_specs=(spec, pl.BlockSpec(memory_space=pl.ANY)),
        scratch_shapes=[
            VMEM((32 * v, 128), jnp.float32),
            VMEM((32 * v, 128), jnp.float32),
            VMEM((8, v, 128), jnp.float32),
            VMEM((3, 8, 16, 128), jnp.float32),
            VMEM((9, 6, 16, 128), jnp.float32),
            VMEM((7, 6, 16, 128), jnp.float32),
            VMEM((7, 11, v, 128), jnp.float32),
            VMEM((5, 9, 3 * v, 128), jnp.float32),
            VMEM((8 * v, 4 * v), jnp.float32),
            pltpu.SemaphoreType.DMA((32,)),
        ],
        compiler_params=pltpu.CompilerParams(vmem_limit_bytes=52 * 2**20),
    )(start, block.reshape(-1, 128), prior.reshape(-1, 128), *pieces, off)


def finish_kernel(scale, total_ref, basis_hbm, new_ref, search_ref, basis_ref, sem):
    v = VECS
    load = pltpu.make_async_copy(basis_hbm, basis_ref, sem)
    load.start()
    coeffs, quotient = ritz_core(total_ref[...])
    coeffs = coeffs * scale
    quotient = jnp.broadcast_to(quotient, (v, 128))
    load.wait()
    for t in range(0, 32, 2):
        basis = []
        for i in (t, t + 1):
            x = basis_ref[i // 8, i % 8]
            search = x[v : 2 * v] - quotient * x[2 * v : 3 * v]
            search_ref[pl.ds(i, v, stride=32), :] = search
            basis.append(jnp.concatenate([x[:v], search, x[3 * v :]], axis=0))
        new = split_dots(coeffs, jnp.concatenate(basis, axis=1), ((1,), (0,)))
        new_ref[pl.ds(t, v, stride=32), :] = new[:, :128]
        new_ref[pl.ds(t + 1, v, stride=32), :] = new[:, 128:]


def finish_call(scale, total, basis):
    v = VECS
    vmem = pl.BlockSpec(memory_space=VMEM)
    out = jax.ShapeDtypeStruct((v * 32, 128), jnp.float32)
    return pl.pallas_call(
        lambda *refs: finish_kernel(scale, *refs),
        out_shape=(out, out),
        in_specs=[vmem, pl.BlockSpec(memory_space=pl.ANY)],
        out_specs=(vmem, vmem),
        scratch_shapes=[VMEM((4, 8, 4 * v, 128), jnp.float32), pltpu.SemaphoreType.DMA],
        compiler_params=pltpu.CompilerParams(vmem_limit_bytes=60 * 2**20),
    )(total, basis)


def spread_sum(rows):
    plane = ("px", "pc")
    count = lax.axis_size("px") * lax.axis_size("pc")
    depth = lax.axis_size("pz")
    pieces = rows.reshape(count, -1, rows.shape[1])
    part = jnp.sum(lax.all_to_all(pieces, plane, 0, 0), axis=0)
    part = jnp.sum(
        lax.all_to_all(jnp.broadcast_to(part[None], (depth,) + part.shape), "pz", 0, 0), axis=0
    )
    whole = lax.all_to_all(jnp.broadcast_to(part[None], (count,) + part.shape), plane, 0, 0)
    return whole.reshape(rows.shape)


def neighbour(payload, step_a, step_b):
    count_a = lax.axis_size("px")
    count_b = lax.axis_size("pz") * lax.axis_size("pc")
    pairs = []
    for a in range(count_a):
        for b in range(count_b):
            if 0 <= a + step_a < count_a and 0 <= b + step_b < count_b:
                pairs.append(((a + step_a) * count_b + b + step_b, a * count_b + b))
    return lax.ppermute(payload, ("px", "pz", "pc"), pairs)


def shards(offsets, block, prior):
    rows_a, rows_b, depth = block.shape[1:]
    total_a = rows_a * lax.axis_size("px")
    total_b = rows_b * lax.axis_size("pz") * lax.axis_size("pc")
    start = jnp.stack(
        [
            lax.axis_index("px") * rows_a,
            lax.axis_index(("pz", "pc")) * rows_b,
            jnp.int32(total_a),
            jnp.int32(total_b),
        ]
    ).astype(jnp.int32)
    down_a, up_a, down_b, up_b = pack_call(block, prior, offsets)
    down_b = neighbour(down_b, 0, 1)
    up_b = neighbour(up_b, 0, -1)
    down_a = neighbour(down_a, 1, 0)
    up_a = neighbour(up_a, -1, 0)
    down_c = neighbour(jnp.concatenate([down_b[:6], up_b[:2]]), 1, 0)
    up_c = neighbour(jnp.concatenate([down_b[12:], down_b[5:6], up_b[2:3], up_b[1:2]]), -1, 0)
    pieces = (down_a, up_a, down_b, up_b, down_c, up_c)
    gram, basis = gram_call(start, block, prior, pieces, offsets)
    scale = math.sqrt(total_a * total_b * depth)
    new_block, search = finish_call(scale, spread_sum(gram), basis)
    return (new_block.reshape(block.shape), search.reshape(block.shape))


def solution(mesh):
    grid = Mesh(
        mesh.devices.reshape(mesh.shape["px"], mesh.shape["py"] // 2, 2), ("px", "pz", "pc")
    )
    spec = P(None, "px", ("pz", "pc"), None)
    return jax.shard_map(
        shards, mesh=grid, in_specs=(spec, spec, spec), out_specs=(spec, spec), check_vma=False
    )
```

```python
import math

import jax
import jax.numpy as jnp
from jax import lax
from jax.experimental import pallas as pl
from jax.experimental.pallas import tpu as pltpu
from jax.sharding import Mesh
from jax.sharding import PartitionSpec as P

VECS = 48
HI = lax.Precision.HIGHEST
FORWARD = [(0, 0, 1), (0, 1, 0), (0, 1, 1), (1, 0, 0), (1, 0, 1), (1, 1, 0), (1, 1, 1)]
VMEM = pltpu.VMEM


def dots(a, b, dims):
    return lax.dot_general(a, b, (dims, ((), ())), precision=HI, preferred_element_type=jnp.float32)


def split(x):
    high = x.astype(jnp.bfloat16)
    return high, (x - high.astype(jnp.float32)).astype(jnp.bfloat16)


def split_dots(a, b, dims):
    (a_high, a_low), (b_high, b_low) = split(a), split(b)
    one = lambda x, y: lax.dot_general(
        x, y, (dims, ((), ())), preferred_element_type=jnp.float32
    )
    return one(a_high, b_high) + (one(a_high, b_low) + one(a_low, b_high))


def pair_factors(first, second, k, place, pivots):
    p = first[k : k + 1, :]
    r = second[k : k + 1, :]
    s = second[k + 1 : k + 2, :]
    inv = 1.0 / (p * s - r * r)
    ratio = r / p
    one = jnp.where(place > k + 1, first * (s * inv) - second * (r * inv), 0.0)
    one = jnp.where(place == k + 1, ratio, one)
    two = jnp.where(place > k + 1, second * (p * inv) - first * (r * inv), 0.0)
    pivots = jnp.where(place == k, p, jnp.where(place == k + 1, s - r * ratio, pivots))
    return one, two, pivots


def eliminated(gram):
    order = gram.shape[0]
    third = order // 3
    rows = lax.broadcasted_iota(jnp.int32, gram.shape, 0)
    cols = lax.broadcasted_iota(jnp.int32, gram.shape, 1)
    inverse = jnp.where(rows == cols, 1.0, 0.0).astype(jnp.float32)
    place = lax.broadcasted_iota(jnp.int32, (third, 128), 0)
    done = []
    for j in range(3):
        left = gram[:third]
        right = inverse[:third]
        gram = gram[third:]
        inverse = inverse[third:]
        pivots = jnp.ones((third, 128), jnp.float32)
        for k in range(0, third, 4):
            c = third * j + k
            columns = [
                jnp.broadcast_to(left[:, c + i : c + i + 1], (third, 128)) for i in range(4)
            ]
            one, two, pivots = pair_factors(columns[0], columns[1], k, place, pivots)
            columns = [
                x - one * x[k : k + 1, :] - two * x[k + 1 : k + 2, :] for x in columns[2:]
            ]
            three, four, pivots = pair_factors(columns[0], columns[1], k + 2, place, pivots)
            one, two, three, four = [
                jnp.concatenate([x, x], axis=1) for x in (one, two, three, four)
            ]
            left = left - one * left[k : k + 1, :] - two * left[k + 1 : k + 2, :]
            right = right - one * right[k : k + 1, :] - two * right[k + 1 : k + 2, :]
            left = left - three * left[k + 2 : k + 3, :] - four * left[k + 3 : k + 4, :]
            right = right - three * right[k + 2 : k + 3, :] - four * right[k + 3 : k + 4, :]
        scale = 1.0 / jnp.sqrt(pivots)
        scale = jnp.concatenate([scale, scale], axis=1)
        left = left * scale
        right = right * scale
        done.append(right)
        if j < 2:
            flipped = left.T[third * (j + 1) : order]
            gram = gram - dots(flipped, left, ((1,), (0,)))
            inverse = inverse - dots(flipped, right, ((1,), (0,)))
    return jnp.concatenate(done, axis=0)


def ritz_core(total):
    vecs = VECS
    order = 3 * vecs
    full = 4 * vecs
    rows = lax.broadcasted_iota(jnp.int32, total.shape, 0)
    cols = lax.broadcasted_iota(jnp.int32, total.shape, 1)
    flipped = total.T
    diagonal = total[full : full + 1, :]
    gram_k = jnp.where(rows <= cols, total, flipped)
    gram_m = jnp.where(rows > cols, total, jnp.where(rows == cols, diagonal, flipped))
    eye = rows == cols
    top = lambda g: jnp.sum(jnp.where(eye, g, 0.0)[:vecs], axis=1, keepdims=True)
    quotient = top(gram_k) / top(gram_m)

    def joined(g):
        mid = g[vecs : 2 * vecs] - quotient * g[2 * vecs : 3 * vecs]
        return jnp.concatenate([g[:vecs], mid, g[3 * vecs : full]], axis=0)

    gram_k = joined(joined(gram_k).T)
    gram_m = joined(joined(gram_m).T)
    gram_m = jnp.concatenate([gram_m, jnp.zeros((order, 256 - order), jnp.float32)], axis=1)
    inverse = eliminated(gram_m)[:, :order]
    half = dots(inverse, gram_k, ((1,), (0,)))
    reduced = dots(half, inverse, ((1,), (1,)))
    bound = jnp.max(jnp.sum(jnp.abs(reduced), axis=1, keepdims=True), axis=0, keepdims=True)
    eye = lax.broadcasted_iota(jnp.int32, (order, order), 0) == lax.broadcasted_iota(
        jnp.int32, (order, order), 1
    )
    shifted = jnp.where(eye, 1.0, 0.0) - reduced / bound
    filtered = dots(shifted[:vecs], shifted, ((1,), (0,)))
    return dots(filtered, inverse, ((1,), (0,))), quotient


def kuhn_tetrahedra():
    orders = [(0, 1, 2), (0, 2, 1), (1, 0, 2), (1, 2, 0), (2, 0, 1), (2, 1, 0)]
    tetrahedra = []
    for ordering in orders:
        corner = [0, 0, 0]
        corners = [(0, 0, 0)]
        for axis_step in ordering:
            corner[axis_step] = 1
            corners.append((corner[0], corner[1], corner[2]))
        tetrahedra.append(corners)
    return tetrahedra


def cross(p, q):
    return (
        p[1] * q[2] - p[2] * q[1],
        p[2] * q[0] - p[0] * q[2],
        p[0] * q[1] - p[1] * q[0],
    )


def dot3(p, q):
    return p[0] * q[0] + p[1] * q[1] + p[2] * q[2]


def shifted_lanes(x, step):
    return pltpu.roll(x, (-step) % x.shape[-1], x.ndim - 1)


def shifted_rows(x, step):
    return pltpu.roll(x, (-step) % x.shape[-2], x.ndim - 2)


def assemble_tables(off_ref, coef_ref, start_a, start_b, total_a, total_b):
    shape = (16, 128)
    row = lax.broadcasted_iota(jnp.int32, shape, 0)
    lane = lax.broadcasted_iota(jnp.int32, shape, 1)
    grid_b = start_b - 2 + row
    valid_bc = (grid_b >= 0) & (grid_b <= total_b - 2) & (row < 11) & (lane < 127)
    coef_ref[...] = jnp.zeros(coef_ref.shape, jnp.float32)

    def plane(a):
        grid_a = (start_a - 2 + a).astype(jnp.float32)
        base = [
            off_ref[0, a] + grid_a,
            off_ref[1, a] + grid_b.astype(jnp.float32),
            off_ref[2, a] + lane.astype(jnp.float32),
        ]
        out = {}
        for db in (0, 1):
            moved = [shifted_rows(p, db) if db else p for p in base]
            for dc in (0, 1):
                out[(db, dc)] = [shifted_lanes(p, dc) if dc else p for p in moved]
        return out

    def add(slot, a, value, b_shift, c_shift):
        if c_shift:
            value = shifted_lanes(value, -1)
        if b_shift == 0:
            value = shifted_rows(value, 1)
        coef_ref[slot, a] = coef_ref[slot, a] + value

    low = plane(0)
    for a in range(7):
        high = plane(a + 1)
        at = lambda corner: (high if corner[0] else low)[(corner[1], corner[2])]
        cell_a = start_a - 2 + a
        inside = valid_bc & (cell_a >= 0) & (cell_a <= total_a - 2)
        sums = {}
        for corners in kuhn_tetrahedra():
            anchor = at(corners[0])
            edges = [tuple(x - y for x, y in zip(at(c), anchor)) for c in corners[1:]]
            g1 = cross(edges[1], edges[2])
            g2 = cross(edges[2], edges[0])
            g3 = cross(edges[0], edges[1])
            g0 = tuple(-(x + y + z) for x, y, z in zip(g1, g2, g3))
            grads = [g0, g1, g2, g3]
            det = jnp.where(inside, jnp.abs(dot3(edges[0], g1)), 1.0)
            weight = jnp.where(inside, 1.0 / (6.0 * det), 0.0)
            for i in range(4):
                for j in range(i, 4):
                    step = tuple(q - p for p, q in zip(corners[i], corners[j]))
                    slot = 7 if i == j else FORWARD.index(step)
                    key = (slot, corners[i])
                    value = dot3(grads[i], grads[j]) * weight
                    sums[key] = sums[key] + value if key in sums else value
            part = jnp.where(inside, det * (1.0 / 24.0), 0.0)
            for corner in corners:
                key = (8, corner)
                sums[key] = sums[key] + part if key in sums else part
        for (slot, corner), value in sums.items():
            table_a = a + corner[0] - 1
            if 0 <= table_a <= 5:
                add(slot, table_a, value, corner[1], corner[2])
        low = high


DOWN_A = [(0, 0), (0, 1), (1, 0), (1, 1), None, None, (0, 7)]
DOWN_A += [(0, b) for b in range(2, 7)] + [(1, b) for b in range(2, 8)]


def pack_kernel(block_ref, prior_ref, off_ref, down_a, up_a, down_b, up_b):
    v = VECS
    block = lambda a, b: block_ref[pl.ds(a * 8 + b, v, stride=32), :]
    prior = lambda a, b: prior_ref[pl.ds(a * 8 + b, v, stride=32), :]
    for a in range(4):
        for b in range(8):
            if a == 2 and b not in (0, 1, 7):
                continue
            x = block(a, b)
            if a == 0 or b == 0:
                y = prior(a, b)
            if a < 2:
                down_a[DOWN_A.index((a, b))] = x
            if a == 0:
                down_a[17 + b if b else 4] = y
            if a == 3:
                up_a[0 if b == 0 else 2 if b == 7 else 2 + b] = x
            if b < 2:
                down_b[b * 4 + a] = x
            if b == 0:
                down_b[8 + a] = y
            if b == 7:
                up_b[a] = x
    for i in range(3):
        for a in range(4):
            down_b[12, i * 8 + a * 2 : i * 8 + a * 2 + 2] = off_ref[i, a, 0:2]
            up_b[4, i * 8 + a * 2 : i * 8 + a * 2 + 2] = off_ref[i, a, 6:8]
        for a in range(2):
            down_a[5, i * 16 + a * 8 : i * 16 + a * 8 + 8] = off_ref[i, a]
            up_a[1, i * 16 + a * 8 : i * 16 + a * 8 + 8] = off_ref[i, 2 + a]


def pack_call(block, prior, offsets):
    v = VECS
    vmem = pl.BlockSpec(memory_space=VMEM)
    sizes = [(n, v, 128) for n in (25, 9, 13, 5)]
    return pl.pallas_call(
        pack_kernel,
        out_shape=tuple(jax.ShapeDtypeStruct(s, jnp.float32) for s in sizes),
        in_specs=[vmem] * 3,
        out_specs=(vmem,) * len(sizes),
        compiler_params=pltpu.CompilerParams(vmem_limit_bytes=60 * 2**20),
    )(block.reshape(-1, 128), prior.reshape(-1, 128), offsets)


def gram_kernel(start_ref, block_hbm, prior_hbm, down_a, up_a, down_b, up_b, down_c, up_c, off_own,
                gram_ref, basis_hbm, block_ref, prior_ref, edge_ref, off_ref, coef_ref, turn_ref, xb_ref, y_ref, acc_ref,
                sems):
    v = VECS
    edges = (down_a.at[5], up_a.at[1], down_b.at[12], up_b.at[4],
             down_c.at[5], up_c.at[3], up_c.at[1], down_c.at[7])
    moves = [(piece, edge_ref.at[i]) for i, piece in enumerate(edges)]
    third = slice(2 * v, 3 * v)
    moves += [(block_hbm, block_ref), (prior_hbm, prior_ref)]
    moves += [
        (down_a.at[0:2], xb_ref.at[5, 1:3]),
        (down_a.at[2:4], xb_ref.at[6, 1:3]),
        (down_a.at[6], xb_ref.at[5, 8]),
        (down_a.at[7:12], xb_ref.at[5, 3:8]),
        (down_a.at[12:18], xb_ref.at[6, 3:9]),
        (up_a.at[0], xb_ref.at[0, 1]),
        (up_a.at[2], xb_ref.at[0, 8]),
        (up_a.at[3:9], xb_ref.at[0, 2:8]),
        (down_b.at[0:4], xb_ref.at[1:5, 9]),
        (down_b.at[4:8], xb_ref.at[1:5, 10]),
        (up_b.at[0:4], xb_ref.at[1:5, 0]),
        (down_c.at[0:2], xb_ref.at[5, 9:11]),
        (down_c.at[2:4], xb_ref.at[6, 9:11]),
        (down_c.at[6], xb_ref.at[0, 9]),
        (up_c.at[0], xb_ref.at[5, 0]),
        (up_c.at[2], xb_ref.at[0, 0]),
        (down_a.at[4], y_ref.at[4, 0, third]),
        (down_a.at[18:25], y_ref.at[4, 1:8, third]),
        (down_b.at[8:12], y_ref.at[0:4, 8, third]),
        (down_c.at[4], y_ref.at[4, 8, third]),
    ]
    copies = [pltpu.make_async_copy(x, y, sems.at[i]) for i, (x, y) in enumerate(moves)]
    for copy in copies:
        copy.start()
    for copy in copies[8:10]:
        copy.wait()
    for a in range(4):
        for b in range(8):
            rows = pl.ds(a * 8 + b, v, stride=32)
            xb_ref[a + 1, b + 1] = block_ref[rows, :]
            y_ref[a, b, third] = prior_ref[rows, :]
    for copy in copies[:8]:
        copy.wait()
    for i in range(3):
        for a in range(4):
            off_ref[i, 2 + a, 2:10] = off_own[i, a]
            pair = slice(i * 8 + a * 2, i * 8 + a * 2 + 2)
            off_ref[i, 2 + a, 10:12] = edge_ref[2, pair]
            off_ref[i, 2 + a, 0:2] = edge_ref[3, pair]
        for a in range(2):
            rows = slice(i * 16 + a * 8, i * 16 + a * 8 + 8)
            off_ref[i, 6 + a, 2:10] = edge_ref[0, rows]
            off_ref[i, a, 2:10] = edge_ref[1, rows]
            low = slice(i * 16 + a * 8, i * 16 + a * 8 + 2)
            high = slice(i * 16 + a * 8 + 6, i * 16 + a * 8 + 8)
            off_ref[i, 6 + a, 10:12] = edge_ref[4, low]
            off_ref[i, a, 0:2] = edge_ref[5, high]
            off_ref[i, 6 + a, 0:2] = edge_ref[6, high]
            off_ref[i, a, 10:12] = edge_ref[7, low]
    assemble_tables(off_ref, coef_ref, start_ref[0], start_ref[1], start_ref[2], start_ref[3])
    for slot, (da, db, dc) in enumerate(FORWARD):
        if dc:
            for a in range(6):
                turn_ref[slot, a] = shifted_lanes(coef_ref[slot, a], -1)
    for copy in copies[10:]:
        copy.wait()

    def row(ref, slot, a, b):
        return ref[slot, a, pl.ds(b, 1), :]

    def k_block(a, b):
        x = lambda i, j: xb_ref[a + 1 + i, b + 1 + j]
        total = x(0, 0) * row(coef_ref, 7, a + 1, b + 1)
        ahead = None
        behind = None
        for slot, (da, db, dc) in enumerate(FORWARD):
            front = x(da, db) * row(turn_ref if dc else coef_ref, slot, a + 1, b + 1)
            back = x(-da, -db) * row(coef_ref, slot, a + 1 - da, b + 1 - db)
            if dc:
                ahead = front if ahead is None else ahead + front
                behind = back if behind is None else behind + back
            else:
                total = total + front + back
        return total + shifted_lanes(ahead, 1) + shifted_lanes(behind, -1)

    def first(t, carry):
        a = t // 9
        b = t - a * 9
        kb = k_block(a, b)
        diagonal = row(coef_ref, 7, a + 1, b + 1)
        inverse = 1.0 / jnp.where(diagonal == 0.0, 1.0, diagonal)
        y_ref[a, b, :v] = kb * inverse
        y_ref[a, b, v : 2 * v] = xb_ref[a + 1, b + 1] * (row(coef_ref, 8, a + 1, b + 1) * inverse)
        return carry

    lax.fori_loop(0, 45, first, 0, unroll=9)
    results = [
        pltpu.make_async_copy(x, basis_hbm.at[:, :, rows], sems.at[30 + i])
        for i, (x, rows) in enumerate(
            ((xb_ref.at[1:5, 1:9], slice(0, v)), (y_ref.at[0:4, 0:8], slice(v, 4 * v)))
        )
    ]
    for copy in results:
        copy.start()

    acc_ref[...] = jnp.zeros(acc_ref.shape, jnp.float32)

    def sides(a, b):
        block = xb_ref[a + 1, b + 1]
        y = y_ref[a, b]
        diagonal = row(coef_ref, 7, a + 1, b + 1)
        mass = row(coef_ref, 8, a + 1, b + 1)
        straight = y * (0.5 * diagonal)
        ahead = None
        for slot, (da, db, dc) in enumerate(FORWARD):
            front = y_ref[a + da, b + db] * row(turn_ref if dc else coef_ref, slot, a + 1, b + 1)
            if dc:
                ahead = front if ahead is None else ahead + front
            else:
                straight = straight + front
        ky = straight + shifted_lanes(ahead, 1)
        kb = y[:v] * diagonal
        basis = jnp.concatenate([block, y], axis=0)
        return basis, jnp.concatenate([kb, ky, basis * mass], axis=0)

    def second(t, carry):
        a = t // 4
        b = (t - a * 4) * 2
        x0, r0 = sides(a, b)
        x1, r1 = sides(a, b + 1)
        left = jnp.concatenate([r0, r1], axis=1)
        right = jnp.concatenate([x0, x1], axis=1)
        acc_ref[...] += split_dots(left, right, ((1,), (1,)))
        return carry

    lax.fori_loop(0, 16, second, 0, unroll=4)

    n = 4 * v
    acc = acc_ref[...]
    pad = lambda g: jnp.concatenate(
        [jnp.concatenate([g, jnp.zeros((n, 256 - n), jnp.float32)], axis=1),
         jnp.zeros((256 - n, 256), jnp.float32)], axis=0)
    half = pad(acc[:n])
    gram_m = pad(acc[n:])
    rows = lax.broadcasted_iota(jnp.int32, (256, 256), 0)
    cols = lax.broadcasted_iota(jnp.int32, (256, 256), 1)
    gram_k = jnp.where(rows < v, half, half + half.T)
    diagonal = jnp.sum(jnp.where(rows == cols, gram_m, 0.0), axis=0, keepdims=True)
    square = jnp.where(rows <= cols, gram_k, gram_m)
    gram_ref[...] = jnp.where(rows < n, square, diagonal)
    for copy in results:
        copy.wait()


def gram_call(start, block, prior, pieces, off):
    v = VECS
    spec = pl.BlockSpec(memory_space=VMEM)
    return pl.pallas_call(
        gram_kernel,
        out_shape=(
            jax.ShapeDtypeStruct((256, 256), jnp.float32),
            jax.ShapeDtypeStruct((4, 8, 4 * v, 128), jnp.float32),
        ),
        in_specs=[pl.BlockSpec(memory_space=pltpu.SMEM)]
        + [pl.BlockSpec(memory_space=pl.ANY)] * (2 + len(pieces))
        + [spec],
        out_specs=(spec, pl.BlockSpec(memory_space=pl.ANY)),
        scratch_shapes=[
            VMEM((32 * v, 128), jnp.float32),
            VMEM((32 * v, 128), jnp.float32),
            VMEM((8, v, 128), jnp.float32),
            VMEM((3, 8, 16, 128), jnp.float32),
            VMEM((9, 6, 16, 128), jnp.float32),
            VMEM((7, 6, 16, 128), jnp.float32),
            VMEM((7, 11, v, 128), jnp.float32),
            VMEM((5, 9, 3 * v, 128), jnp.float32),
            VMEM((8 * v, 4 * v), jnp.float32),
            pltpu.SemaphoreType.DMA((32,)),
        ],
        compiler_params=pltpu.CompilerParams(vmem_limit_bytes=52 * 2**20),
    )(start, block.reshape(-1, 128), prior.reshape(-1, 128), *pieces, off)


def finish_kernel(scale, total_ref, basis_hbm, new_ref, search_ref, basis_ref, sem):
    v = VECS
    load = pltpu.make_async_copy(basis_hbm, basis_ref, sem)
    load.start()
    coeffs, quotient = ritz_core(total_ref[...])
    coeffs = coeffs * scale
    quotient = jnp.broadcast_to(quotient, (v, 128))
    load.wait()
    for t in range(0, 32, 2):
        basis = []
        for i in (t, t + 1):
            x = basis_ref[i // 8, i % 8]
            search = x[v : 2 * v] - quotient * x[2 * v : 3 * v]
            search_ref[pl.ds(i, v, stride=32), :] = search
            basis.append(jnp.concatenate([x[:v], search, x[3 * v :]], axis=0))
        new = split_dots(coeffs, jnp.concatenate(basis, axis=1), ((1,), (0,)))
        new_ref[pl.ds(t, v, stride=32), :] = new[:, :128]
        new_ref[pl.ds(t + 1, v, stride=32), :] = new[:, 128:]


def finish_call(scale, total, basis):
    v = VECS
    vmem = pl.BlockSpec(memory_space=VMEM)
    out = jax.ShapeDtypeStruct((v * 32, 128), jnp.float32)
    return pl.pallas_call(
        lambda *refs: finish_kernel(scale, *refs),
        out_shape=(out, out),
        in_specs=[vmem, pl.BlockSpec(memory_space=pl.ANY)],
        out_specs=(vmem, vmem),
        scratch_shapes=[VMEM((4, 8, 4 * v, 128), jnp.float32), pltpu.SemaphoreType.DMA],
        compiler_params=pltpu.CompilerParams(vmem_limit_bytes=60 * 2**20),
    )(total, basis)


def spread_sum(rows):
    plane = ("px", "pc")
    count = lax.axis_size("px") * lax.axis_size("pc")
    depth = lax.axis_size("pz")
    pieces = rows.reshape(count, -1, rows.shape[1])
    part = jnp.sum(lax.all_to_all(pieces, plane, 0, 0), axis=0)
    part = jnp.sum(
        lax.all_to_all(jnp.broadcast_to(part[None], (depth,) + part.shape), "pz", 0, 0), axis=0
    )
    whole = lax.all_to_all(jnp.broadcast_to(part[None], (count,) + part.shape), plane, 0, 0)
    return whole.reshape(rows.shape)


def neighbour(payload, step_a, step_b):
    count_a = lax.axis_size("px")
    count_b = lax.axis_size("pz") * lax.axis_size("pc")
    pairs = []
    for a in range(count_a):
        for b in range(count_b):
            if 0 <= a + step_a < count_a and 0 <= b + step_b < count_b:
                pairs.append(((a + step_a) * count_b + b + step_b, a * count_b + b))
    return lax.ppermute(payload, ("px", "pz", "pc"), pairs)


def shards(offsets, block, prior):
    rows_a, rows_b, depth = block.shape[1:]
    total_a = rows_a * lax.axis_size("px")
    total_b = rows_b * lax.axis_size("pz") * lax.axis_size("pc")
    start = jnp.stack(
        [
            lax.axis_index("px") * rows_a,
            lax.axis_index(("pz", "pc")) * rows_b,
            jnp.int32(total_a),
            jnp.int32(total_b),
        ]
    ).astype(jnp.int32)
    down_a, up_a, down_b, up_b = pack_call(block, prior, offsets)
    down_b = neighbour(down_b, 0, 1)
    up_b = neighbour(up_b, 0, -1)
    down_a = neighbour(down_a, 1, 0)
    up_a = neighbour(up_a, -1, 0)
    down_c = neighbour(jnp.concatenate([down_a[:6], up_a[:2]]), 0, 1)
    up_c = neighbour(jnp.concatenate([down_a[6:7], down_a[5:6], up_a[2:3], up_a[1:2]]), 0, -1)
    pieces = (down_a, up_a, down_b, up_b, down_c, up_c)
    gram, basis = gram_call(start, block, prior, pieces, offsets)
    scale = math.sqrt(total_a * total_b * depth)
    new_block, search = finish_call(scale, spread_sum(gram), basis)
    return (new_block.reshape(block.shape), search.reshape(block.shape))


def solution(mesh):
    grid = Mesh(
        mesh.devices.reshape(mesh.shape["px"], mesh.shape["py"] // 2, 2), ("px", "pz", "pc")
    )
    spec = P(None, "px", ("pz", "pc"), None)
    return jax.shard_map(
        shards, mesh=grid, in_specs=(spec, spec, spec), out_specs=(spec, spec), check_vma=False
    )
```

```python
import math

import jax
import jax.numpy as jnp
from jax import lax
from jax.experimental import pallas as pl
from jax.experimental.pallas import tpu as pltpu
from jax.sharding import Mesh
from jax.sharding import PartitionSpec as P

VECS = 48
HI = lax.Precision.HIGHEST
FORWARD = [(0, 0, 1), (0, 1, 0), (0, 1, 1), (1, 0, 0), (1, 0, 1), (1, 1, 0), (1, 1, 1)]
VMEM = pltpu.VMEM


def dots(a, b, dims):
    return lax.dot_general(a, b, (dims, ((), ())), precision=HI, preferred_element_type=jnp.float32)


def split(x):
    high = x.astype(jnp.bfloat16)
    return high, (x - high.astype(jnp.float32)).astype(jnp.bfloat16)


def split_dots(a, b, dims):
    (a_high, a_low), (b_high, b_low) = split(a), split(b)
    one = lambda x, y: lax.dot_general(
        x, y, (dims, ((), ())), preferred_element_type=jnp.float32
    )
    return one(a_high, b_high) + (one(a_high, b_low) + one(a_low, b_high))


def pair_factors(first, second, k, place, pivots):
    p = first[k : k + 1, :]
    r = second[k : k + 1, :]
    s = second[k + 1 : k + 2, :]
    inv = 1.0 / (p * s - r * r)
    ratio = r / p
    one = jnp.where(place > k + 1, first * (s * inv) - second * (r * inv), 0.0)
    one = jnp.where(place == k + 1, ratio, one)
    two = jnp.where(place > k + 1, second * (p * inv) - first * (r * inv), 0.0)
    pivots = jnp.where(place == k, p, jnp.where(place == k + 1, s - r * ratio, pivots))
    return one, two, pivots


def eliminated(gram):
    order = gram.shape[0]
    third = order // 3
    rows = lax.broadcasted_iota(jnp.int32, gram.shape, 0)
    cols = lax.broadcasted_iota(jnp.int32, gram.shape, 1)
    inverse = jnp.where(rows == cols, 1.0, 0.0).astype(jnp.float32)
    place = lax.broadcasted_iota(jnp.int32, (third, 128), 0)
    done = []
    for j in range(3):
        left = gram[:third]
        right = inverse[:third]
        gram = gram[third:]
        inverse = inverse[third:]
        pivots = jnp.ones((third, 128), jnp.float32)
        for k in range(0, third, 4):
            c = third * j + k
            columns = [
                jnp.broadcast_to(left[:, c + i : c + i + 1], (third, 128)) for i in range(4)
            ]
            one, two, pivots = pair_factors(columns[0], columns[1], k, place, pivots)
            columns = [
                x - one * x[k : k + 1, :] - two * x[k + 1 : k + 2, :] for x in columns[2:]
            ]
            three, four, pivots = pair_factors(columns[0], columns[1], k + 2, place, pivots)
            one, two, three, four = [
                jnp.concatenate([x, x], axis=1) for x in (one, two, three, four)
            ]
            left = left - one * left[k : k + 1, :] - two * left[k + 1 : k + 2, :]
            right = right - one * right[k : k + 1, :] - two * right[k + 1 : k + 2, :]
            left = left - three * left[k + 2 : k + 3, :] - four * left[k + 3 : k + 4, :]
            right = right - three * right[k + 2 : k + 3, :] - four * right[k + 3 : k + 4, :]
        scale = 1.0 / jnp.sqrt(pivots)
        scale = jnp.concatenate([scale, scale], axis=1)
        left = left * scale
        right = right * scale
        done.append(right)
        if j < 2:
            flipped = left.T[third * (j + 1) : order]
            gram = gram - dots(flipped, left, ((1,), (0,)))
            inverse = inverse - dots(flipped, right, ((1,), (0,)))
    return jnp.concatenate(done, axis=0)


def ritz_core(total):
    vecs = VECS
    order = 3 * vecs
    full = 4 * vecs
    rows = lax.broadcasted_iota(jnp.int32, total.shape, 0)
    cols = lax.broadcasted_iota(jnp.int32, total.shape, 1)
    flipped = total.T
    diagonal = total[full : full + 1, :]
    gram_k = jnp.where(rows <= cols, total, flipped)
    gram_m = jnp.where(rows > cols, total, jnp.where(rows == cols, diagonal, flipped))
    eye = rows == cols
    top = lambda g: jnp.sum(jnp.where(eye, g, 0.0)[:vecs], axis=1, keepdims=True)
    quotient = top(gram_k) / top(gram_m)

    def joined(g):
        mid = g[vecs : 2 * vecs] - quotient * g[2 * vecs : 3 * vecs]
        return jnp.concatenate([g[:vecs], mid, g[3 * vecs : full]], axis=0)

    gram_k = joined(joined(gram_k).T)
    gram_m = joined(joined(gram_m).T)
    gram_m = jnp.concatenate([gram_m, jnp.zeros((order, 256 - order), jnp.float32)], axis=1)
    inverse = eliminated(gram_m)[:, :order]
    half = dots(inverse, gram_k, ((1,), (0,)))
    reduced = dots(half, inverse, ((1,), (1,)))
    bound = jnp.max(jnp.sum(jnp.abs(reduced), axis=1, keepdims=True), axis=0, keepdims=True)
    eye = lax.broadcasted_iota(jnp.int32, (order, order), 0) == lax.broadcasted_iota(
        jnp.int32, (order, order), 1
    )
    shifted = jnp.where(eye, 1.0, 0.0) - reduced / bound
    filtered = dots(shifted[:vecs], shifted, ((1,), (0,)))
    return dots(filtered, inverse, ((1,), (0,))), quotient


def kuhn_tetrahedra():
    orders = [(0, 1, 2), (0, 2, 1), (1, 0, 2), (1, 2, 0), (2, 0, 1), (2, 1, 0)]
    tetrahedra = []
    for ordering in orders:
        corner = [0, 0, 0]
        corners = [(0, 0, 0)]
        for axis_step in ordering:
            corner[axis_step] = 1
            corners.append((corner[0], corner[1], corner[2]))
        tetrahedra.append(corners)
    return tetrahedra


def cross(p, q):
    return (
        p[1] * q[2] - p[2] * q[1],
        p[2] * q[0] - p[0] * q[2],
        p[0] * q[1] - p[1] * q[0],
    )


def dot3(p, q):
    return p[0] * q[0] + p[1] * q[1] + p[2] * q[2]


def shifted_lanes(x, step):
    return pltpu.roll(x, (-step) % x.shape[-1], x.ndim - 1)


def shifted_rows(x, step):
    return pltpu.roll(x, (-step) % x.shape[-2], x.ndim - 2)


def assemble_tables(off_ref, coef_ref, start_a, start_b, total_a, total_b):
    shape = (16, 128)
    row = lax.broadcasted_iota(jnp.int32, shape, 0)
    lane = lax.broadcasted_iota(jnp.int32, shape, 1)
    grid_b = start_b - 2 + row
    valid_bc = (grid_b >= 0) & (grid_b <= total_b - 2) & (row < 11) & (lane < 127)
    coef_ref[...] = jnp.zeros(coef_ref.shape, jnp.float32)

    def plane(a):
        grid_a = (start_a - 2 + a).astype(jnp.float32)
        base = [
            off_ref[0, a] + grid_a,
            off_ref[1, a] + grid_b.astype(jnp.float32),
            off_ref[2, a] + lane.astype(jnp.float32),
        ]
        out = {}
        for db in (0, 1):
            moved = [shifted_rows(p, db) if db else p for p in base]
            for dc in (0, 1):
                out[(db, dc)] = [shifted_lanes(p, dc) if dc else p for p in moved]
        return out

    def add(slot, a, value, b_shift, c_shift):
        if c_shift:
            value = shifted_lanes(value, -1)
        if b_shift == 0:
            value = shifted_rows(value, 1)
        coef_ref[slot, a] = coef_ref[slot, a] + value

    low = plane(0)
    for a in range(7):
        high = plane(a + 1)
        at = lambda corner: (high if corner[0] else low)[(corner[1], corner[2])]
        cell_a = start_a - 2 + a
        inside = valid_bc & (cell_a >= 0) & (cell_a <= total_a - 2)
        sums = {}
        for corners in kuhn_tetrahedra():
            anchor = at(corners[0])
            edges = [tuple(x - y for x, y in zip(at(c), anchor)) for c in corners[1:]]
            g1 = cross(edges[1], edges[2])
            g2 = cross(edges[2], edges[0])
            g3 = cross(edges[0], edges[1])
            g0 = tuple(-(x + y + z) for x, y, z in zip(g1, g2, g3))
            grads = [g0, g1, g2, g3]
            det = jnp.where(inside, jnp.abs(dot3(edges[0], g1)), 1.0)
            weight = jnp.where(inside, 1.0 / (6.0 * det), 0.0)
            for i in range(4):
                for j in range(i, 4):
                    step = tuple(q - p for p, q in zip(corners[i], corners[j]))
                    slot = 7 if i == j else FORWARD.index(step)
                    key = (slot, corners[i])
                    value = dot3(grads[i], grads[j]) * weight
                    sums[key] = sums[key] + value if key in sums else value
            part = jnp.where(inside, det * (1.0 / 24.0), 0.0)
            for corner in corners:
                key = (8, corner)
                sums[key] = sums[key] + part if key in sums else part
        for (slot, corner), value in sums.items():
            table_a = a + corner[0] - 1
            if 0 <= table_a <= 5:
                add(slot, table_a, value, corner[1], corner[2])
        low = high


DOWN_A = [(0, 0), (0, 1), (1, 0), (1, 1), None, None, (0, 7)]
DOWN_A += [(0, b) for b in range(2, 7)] + [(1, b) for b in range(2, 8)]


def pack_kernel(block_ref, prior_ref, off_ref, down_a, up_a, down_b, up_b):
    v = VECS
    block = lambda a, b: block_ref[pl.ds(a * 8 + b, v, stride=32), :]
    prior = lambda a, b: prior_ref[pl.ds(a * 8 + b, v, stride=32), :]
    for a in range(4):
        for b in range(8):
            if a == 2 and b not in (0, 1, 7):
                continue
            x = block(a, b)
            if a == 0 or b == 0:
                y = prior(a, b)
            if a < 2:
                down_a[DOWN_A.index((a, b))] = x
            if a == 0:
                down_a[17 + b if b else 4] = y
            if a == 3:
                up_a[0 if b == 0 else 2 if b == 7 else 2 + b] = x
            if b < 2:
                down_b[b * 4 + a] = x
            if b == 0:
                down_b[8 + a] = y
            if b == 7:
                up_b[a] = x
    for i in range(3):
        for a in range(4):
            down_b[12, i * 8 + a * 2 : i * 8 + a * 2 + 2] = off_ref[i, a, 0:2]
            up_b[4, i * 8 + a * 2 : i * 8 + a * 2 + 2] = off_ref[i, a, 6:8]
        for a in range(2):
            down_a[5, i * 16 + a * 8 : i * 16 + a * 8 + 8] = off_ref[i, a]
            up_a[1, i * 16 + a * 8 : i * 16 + a * 8 + 8] = off_ref[i, 2 + a]


def pack_call(block, prior, offsets):
    v = VECS
    vmem = pl.BlockSpec(memory_space=VMEM)
    sizes = [(n, v, 128) for n in (25, 9, 13, 5)]
    return pl.pallas_call(
        pack_kernel,
        out_shape=tuple(jax.ShapeDtypeStruct(s, jnp.float32) for s in sizes),
        in_specs=[vmem] * 3,
        out_specs=(vmem,) * len(sizes),
        compiler_params=pltpu.CompilerParams(vmem_limit_bytes=60 * 2**20),
    )(block.reshape(-1, 128), prior.reshape(-1, 128), offsets)


def gram_kernel(start_ref, block_hbm, prior_hbm, down_a, up_a, down_b, up_b, down_c, up_c, off_hbm,
                gram_ref, basis_hbm, block_ref, prior_ref, off_own, edge_ref, off_ref, coef_ref, turn_ref, xb_ref, y_ref, acc_ref,
                sems):
    v = VECS
    edges = (down_a.at[5], up_a.at[1], down_b.at[12], up_b.at[4],
             down_c.at[5], up_c.at[3], up_c.at[1], down_c.at[7])
    moves = [(piece, edge_ref.at[i]) for i, piece in enumerate(edges)]
    third = slice(2 * v, 3 * v)
    moves += [(block_hbm, block_ref), (prior_hbm, prior_ref)]
    moves += [
        (down_a.at[0:2], xb_ref.at[5, 1:3]),
        (down_a.at[2:4], xb_ref.at[6, 1:3]),
        (down_a.at[6], xb_ref.at[5, 8]),
        (down_a.at[7:12], xb_ref.at[5, 3:8]),
        (down_a.at[12:18], xb_ref.at[6, 3:9]),
        (up_a.at[0], xb_ref.at[0, 1]),
        (up_a.at[2], xb_ref.at[0, 8]),
        (up_a.at[3:9], xb_ref.at[0, 2:8]),
        (down_b.at[0:4], xb_ref.at[1:5, 9]),
        (down_b.at[4:8], xb_ref.at[1:5, 10]),
        (up_b.at[0:4], xb_ref.at[1:5, 0]),
        (down_c.at[0:2], xb_ref.at[5, 9:11]),
        (down_c.at[2:4], xb_ref.at[6, 9:11]),
        (down_c.at[6], xb_ref.at[0, 9]),
        (up_c.at[0], xb_ref.at[5, 0]),
        (up_c.at[2], xb_ref.at[0, 0]),
        (down_a.at[4], y_ref.at[4, 0, third]),
        (down_a.at[18:25], y_ref.at[4, 1:8, third]),
        (down_b.at[8:12], y_ref.at[0:4, 8, third]),
        (down_c.at[4], y_ref.at[4, 8, third]),
    ]
    copies = [pltpu.make_async_copy(x, y, sems.at[i]) for i, (x, y) in enumerate(moves)]
    own_offsets = pltpu.make_async_copy(off_hbm, off_own, sems.at[32])
    own_offsets.start()
    for copy in copies:
        copy.start()
    for copy in copies[8:10]:
        copy.wait()
    for a in range(4):
        for b in range(8):
            rows = pl.ds(a * 8 + b, v, stride=32)
            xb_ref[a + 1, b + 1] = block_ref[rows, :]
            y_ref[a, b, third] = prior_ref[rows, :]
    own_offsets.wait()
    for copy in copies[:8]:
        copy.wait()
    for i in range(3):
        for a in range(4):
            off_ref[i, 2 + a, 2:10] = off_own[i, a]
            pair = slice(i * 8 + a * 2, i * 8 + a * 2 + 2)
            off_ref[i, 2 + a, 10:12] = edge_ref[2, pair]
            off_ref[i, 2 + a, 0:2] = edge_ref[3, pair]
        for a in range(2):
            rows = slice(i * 16 + a * 8, i * 16 + a * 8 + 8)
            off_ref[i, 6 + a, 2:10] = edge_ref[0, rows]
            off_ref[i, a, 2:10] = edge_ref[1, rows]
            low = slice(i * 16 + a * 8, i * 16 + a * 8 + 2)
            high = slice(i * 16 + a * 8 + 6, i * 16 + a * 8 + 8)
            off_ref[i, 6 + a, 10:12] = edge_ref[4, low]
            off_ref[i, a, 0:2] = edge_ref[5, high]
            off_ref[i, 6 + a, 0:2] = edge_ref[6, high]
            off_ref[i, a, 10:12] = edge_ref[7, low]
    assemble_tables(off_ref, coef_ref, start_ref[0], start_ref[1], start_ref[2], start_ref[3])
    for slot, (da, db, dc) in enumerate(FORWARD):
        if dc:
            for a in range(6):
                turn_ref[slot, a] = shifted_lanes(coef_ref[slot, a], -1)
    for copy in copies[10:]:
        copy.wait()

    def row(ref, slot, a, b):
        return ref[slot, a, pl.ds(b, 1), :]

    def k_block(a, b):
        x = lambda i, j: xb_ref[a + 1 + i, b + 1 + j]
        total = x(0, 0) * row(coef_ref, 7, a + 1, b + 1)
        ahead = None
        behind = None
        for slot, (da, db, dc) in enumerate(FORWARD):
            front = x(da, db) * row(turn_ref if dc else coef_ref, slot, a + 1, b + 1)
            back = x(-da, -db) * row(coef_ref, slot, a + 1 - da, b + 1 - db)
            if dc:
                ahead = front if ahead is None else ahead + front
                behind = back if behind is None else behind + back
            else:
                total = total + front + back
        return total + shifted_lanes(ahead, 1) + shifted_lanes(behind, -1)

    def first(t, carry):
        a = t // 9
        b = t - a * 9
        kb = k_block(a, b)
        diagonal = row(coef_ref, 7, a + 1, b + 1)
        inverse = 1.0 / jnp.where(diagonal == 0.0, 1.0, diagonal)
        y_ref[a, b, :v] = kb * inverse
        y_ref[a, b, v : 2 * v] = xb_ref[a + 1, b + 1] * (row(coef_ref, 8, a + 1, b + 1) * inverse)
        return carry

    lax.fori_loop(0, 45, first, 0, unroll=9)
    results = [
        pltpu.make_async_copy(x, basis_hbm.at[:, :, rows], sems.at[30 + i])
        for i, (x, rows) in enumerate(
            ((xb_ref.at[1:5, 1:9], slice(0, v)), (y_ref.at[0:4, 0:8], slice(v, 4 * v)))
        )
    ]
    for copy in results:
        copy.start()

    acc_ref[...] = jnp.zeros(acc_ref.shape, jnp.float32)

    def sides(a, b):
        block = xb_ref[a + 1, b + 1]
        y = y_ref[a, b]
        diagonal = row(coef_ref, 7, a + 1, b + 1)
        mass = row(coef_ref, 8, a + 1, b + 1)
        straight = y * (0.5 * diagonal)
        ahead = None
        for slot, (da, db, dc) in enumerate(FORWARD):
            front = y_ref[a + da, b + db] * row(turn_ref if dc else coef_ref, slot, a + 1, b + 1)
            if dc:
                ahead = front if ahead is None else ahead + front
            else:
                straight = straight + front
        ky = straight + shifted_lanes(ahead, 1)
        kb = y[:v] * diagonal
        basis = jnp.concatenate([block, y], axis=0)
        return basis, jnp.concatenate([kb, ky, basis * mass], axis=0)

    def second(t, carry):
        a = t // 4
        b = (t - a * 4) * 2
        x0, r0 = sides(a, b)
        x1, r1 = sides(a, b + 1)
        left = jnp.concatenate([r0, r1], axis=1)
        right = jnp.concatenate([x0, x1], axis=1)
        acc_ref[...] += split_dots(left, right, ((1,), (1,)))
        return carry

    lax.fori_loop(0, 16, second, 0, unroll=8)

    n = 4 * v
    acc = acc_ref[...]
    pad = lambda g: jnp.concatenate(
        [jnp.concatenate([g, jnp.zeros((n, 256 - n), jnp.float32)], axis=1),
         jnp.zeros((256 - n, 256), jnp.float32)], axis=0)
    half = pad(acc[:n])
    gram_m = pad(acc[n:])
    rows = lax.broadcasted_iota(jnp.int32, (256, 256), 0)
    cols = lax.broadcasted_iota(jnp.int32, (256, 256), 1)
    gram_k = jnp.where(rows < v, half, half + half.T)
    diagonal = jnp.sum(jnp.where(rows == cols, gram_m, 0.0), axis=0, keepdims=True)
    square = jnp.where(rows <= cols, gram_k, gram_m)
    gram_ref[...] = jnp.where(rows < n, square, diagonal)
    for copy in results:
        copy.wait()


def gram_call(start, block, prior, pieces, off):
    v = VECS
    spec = pl.BlockSpec(memory_space=VMEM)
    return pl.pallas_call(
        gram_kernel,
        out_shape=(
            jax.ShapeDtypeStruct((256, 256), jnp.float32),
            jax.ShapeDtypeStruct((4, 8, 4 * v, 128), jnp.float32),
        ),
        in_specs=[pl.BlockSpec(memory_space=pltpu.SMEM)]
        + [pl.BlockSpec(memory_space=pl.ANY)] * (3 + len(pieces)),
        out_specs=(spec, pl.BlockSpec(memory_space=pl.ANY)),
        scratch_shapes=[
            VMEM((32 * v, 128), jnp.float32),
            VMEM((32 * v, 128), jnp.float32),
            VMEM((3, 4, 8, 128), jnp.float32),
            VMEM((8, v, 128), jnp.float32),
            VMEM((3, 8, 16, 128), jnp.float32),
            VMEM((9, 6, 16, 128), jnp.float32),
            VMEM((7, 6, 16, 128), jnp.float32),
            VMEM((7, 11, v, 128), jnp.float32),
            VMEM((5, 9, 3 * v, 128), jnp.float32),
            VMEM((8 * v, 4 * v), jnp.float32),
            pltpu.SemaphoreType.DMA((33,)),
        ],
        compiler_params=pltpu.CompilerParams(vmem_limit_bytes=52 * 2**20),
    )(start, block.reshape(-1, 128), prior.reshape(-1, 128), *pieces, off)


def finish_kernel(scale, total_ref, basis_hbm, new_ref, search_ref, basis_ref, sem):
    v = VECS
    load = pltpu.make_async_copy(basis_hbm, basis_ref, sem)
    load.start()
    coeffs, quotient = ritz_core(total_ref[...])
    coeffs = coeffs * scale
    quotient = jnp.broadcast_to(quotient, (v, 128))
    load.wait()
    for t in range(0, 32, 2):
        basis = []
        for i in (t, t + 1):
            x = basis_ref[i // 8, i % 8]
            search = x[v : 2 * v] - quotient * x[2 * v : 3 * v]
            search_ref[pl.ds(i, v, stride=32), :] = search
            basis.append(jnp.concatenate([x[:v], search, x[3 * v :]], axis=0))
        new = split_dots(coeffs, jnp.concatenate(basis, axis=1), ((1,), (0,)))
        new_ref[pl.ds(t, v, stride=32), :] = new[:, :128]
        new_ref[pl.ds(t + 1, v, stride=32), :] = new[:, 128:]


def finish_call(scale, total, basis):
    v = VECS
    vmem = pl.BlockSpec(memory_space=VMEM)
    out = jax.ShapeDtypeStruct((v * 32, 128), jnp.float32)
    return pl.pallas_call(
        lambda *refs: finish_kernel(scale, *refs),
        out_shape=(out, out),
        in_specs=[vmem, pl.BlockSpec(memory_space=pl.ANY)],
        out_specs=(vmem, vmem),
        scratch_shapes=[VMEM((4, 8, 4 * v, 128), jnp.float32), pltpu.SemaphoreType.DMA],
        compiler_params=pltpu.CompilerParams(vmem_limit_bytes=60 * 2**20),
    )(total, basis)


def spread_sum(rows):
    plane = ("px", "pc")
    count = lax.axis_size("px") * lax.axis_size("pc")
    depth = lax.axis_size("pz")
    pieces = rows.reshape(count, -1, rows.shape[1])
    part = jnp.sum(lax.all_to_all(pieces, plane, 0, 0), axis=0)
    part = jnp.sum(
        lax.all_to_all(jnp.broadcast_to(part[None], (depth,) + part.shape), "pz", 0, 0), axis=0
    )
    whole = lax.all_to_all(jnp.broadcast_to(part[None], (count,) + part.shape), plane, 0, 0)
    return whole.reshape(rows.shape)


def neighbour(payload, step_a, step_b):
    count_a = lax.axis_size("px")
    count_b = lax.axis_size("pz") * lax.axis_size("pc")
    pairs = []
    for a in range(count_a):
        for b in range(count_b):
            if 0 <= a + step_a < count_a and 0 <= b + step_b < count_b:
                pairs.append(((a + step_a) * count_b + b + step_b, a * count_b + b))
    return lax.ppermute(payload, ("px", "pz", "pc"), pairs)


def shards(offsets, block, prior):
    rows_a, rows_b, depth = block.shape[1:]
    total_a = rows_a * lax.axis_size("px")
    total_b = rows_b * lax.axis_size("pz") * lax.axis_size("pc")
    start = jnp.stack(
        [
            lax.axis_index("px") * rows_a,
            lax.axis_index(("pz", "pc")) * rows_b,
            jnp.int32(total_a),
            jnp.int32(total_b),
        ]
    ).astype(jnp.int32)
    down_a, up_a, down_b, up_b = pack_call(block, prior, offsets)
    down_b = neighbour(down_b, 0, 1)
    up_b = neighbour(up_b, 0, -1)
    down_a = neighbour(down_a, 1, 0)
    up_a = neighbour(up_a, -1, 0)
    down_c = neighbour(jnp.concatenate([down_a[:6], up_a[:2]]), 0, 1)
    up_c = neighbour(jnp.concatenate([down_a[6:7], down_a[5:6], up_a[2:3], up_a[1:2]]), 0, -1)
    pieces = (down_a, up_a, down_b, up_b, down_c, up_c)
    gram, basis = gram_call(start, block, prior, pieces, offsets)
    scale = math.sqrt(total_a * total_b * depth)
    new_block, search = finish_call(scale, spread_sum(gram), basis)
    return (new_block.reshape(block.shape), search.reshape(block.shape))


def solution(mesh):
    grid = Mesh(
        mesh.devices.reshape(mesh.shape["px"], mesh.shape["py"] // 2, 2), ("px", "pz", "pc")
    )
    spec = P(None, "px", ("pz", "pc"), None)
    return jax.shard_map(
        shards, mesh=grid, in_specs=(spec, spec, spec), out_specs=(spec, spec), check_vma=False
    )
```
